512 devices in a mesh: grp: 64 (over z, x), sub: 4 (over y), rep: 2 (over core).
Axes of the slice: x: 4, y: 4, z: 16, core: 2. Of those that a mesh axis runs over, the one named last changes fastest.
Arguments:
- starting_concentration_per_run: float32 [64, 8, 256, 512], P('grp', None, 'sub', 'rep'), may hold values from -6 to 6
- diffusivity: float32 [256, 512], P('sub', 'rep'), may hold values from 0.02 to 0.12
- run_layer_stability_number: float32 [64, 8], P('grp'), may hold values from 0.05 to 0.4
- observed: float32 [256, 4, 128], P(('sub', 'grp'), 'rep'), may hold values from -6 to 6
- slot_error_variance: float32 [256, 4, 128], P(('sub', 'grp'), 'rep'), may hold values from 0.25 to 4
- sensor_target_site: int32 [256, 4, 128], P(('sub', 'grp'), 'rep'), may hold values from 0 to 1023
- patch_live_count: int32 [256, 4], P(('sub', 'grp'), 'rep'), may hold values from 1 to 128, as said below
Outputs:
- analysis: float32 [64, 8, 256, 512], P('grp', None, 'sub', 'rep')
The draws below stay inside these ranges and needn't reach their ends.
Inputs may be any that keep to these rules, and one draw needn't show every extreme that they name: Slots below patch_live_count of a patch are live, the rest are unused; some patch has all 128 slots live. `sensor_target_site`: A slot observes the cell level * 128 + column of its own patch.
All inputs are finite; a program needn't handle non-finite values.
Results may differ from the reference program's by a relative error of at most 0.0003.
Values sent between devices are 32-bit elements; how exact they have to be, the bound alone decides.
No kernel may reach another device: no remote copies, remote signals or barrier semaphores. Data moves between devices by JAX's collectives and lax.ppermute only.
A program may use at most 64 MiB of HBM per device.

```python
import math
import jax
import jax.numpy as jnp
from jax import lax

VERTICAL_LEVELS = 8
PATCH = 128
SLOTS = 128
STEPS = 4
NS_ITERS = 4
ENSEMBLE_SIZE = 64
GRID_ROWS = 256
GRID_COLUMNS = 512
NXP = 4


def draw_patch_live_count(key, part):
    first_key, second_key = jax.random.split(jax.random.fold_in(key, 11))
    uniform_int = jax.random.randint(first_key, (GRID_ROWS * NXP,), 0, 1024)
    cubed = uniform_int * uniform_int // 1024 * uniform_int // 1024
    counts = 1 + cubed * (SLOTS - 1) // 1023
    position = jax.random.randint(second_key, (), 0, GRID_ROWS * NXP)
    counts = counts.at[position].set(SLOTS)
    return counts.reshape(GRID_ROWS, NXP).astype(jnp.int32)


def with_ends(array, key, low, high):
    extent = array.shape
    place = [jax.random.randint(jax.random.fold_in(key, axis), (), 0, extent[axis]) for axis in range(len(extent))]
    array = array.at[tuple(place)].set(low)
    longest = extent.index(max(extent))
    place[longest] = (place[longest] + 1) % extent[longest]
    return array.at[tuple(place)].set(high)


def shard_levels(own_key, extent, cuts, low, high):
    loudness = 1.0
    for dim, shards_of in cuts:
        draws = jax.random.uniform(jax.random.fold_in(jax.random.fold_in(own_key, 6), dim), (shards_of,), jnp.float32, low / len(cuts), high / len(cuts))
        loudness = loudness * jnp.repeat(jnp.exp(draws), extent[dim] // shards_of).reshape((-1,) + (1,) * (len(extent) - 1 - dim))
    return loudness


def centred(stream_key, shape, width, most, cuts=(), kind=jnp.bfloat16):
    drawn = width * jax.random.normal(stream_key, shape, jnp.float32)
    if cuts:
        drawn = drawn * shard_levels(stream_key, shape, cuts, -0.22, 0.18)
    return jnp.clip(drawn, -most, most).astype(kind)


def setup_inputs(seed: int = 0) -> dict:
    keys = jax.random.split(jax.random.key(seed), 8)
    starting_concentration_per_run = centred(keys[0], (ENSEMBLE_SIZE, VERTICAL_LEVELS, GRID_ROWS, GRID_COLUMNS), 1.0, 6.0, ((0, 64), (2, 4), (3, 2)), jnp.float32)
    diffusivity = jnp.clip(jnp.exp(math.log(0.12) - 1.7917595 * jax.random.uniform(keys[1], (GRID_ROWS, GRID_COLUMNS), jnp.float32) ** shard_levels(keys[1], (GRID_ROWS, GRID_COLUMNS), ((0, 4), (1, 2)), -0.2, 0.2)), 0.02, 0.12)
    run_layer_stability_number = jnp.clip(jnp.exp(math.log(0.4) - 2.0794415 * jax.random.uniform(keys[2], (ENSEMBLE_SIZE, VERTICAL_LEVELS), jnp.float32) ** shard_levels(keys[2], (ENSEMBLE_SIZE, VERTICAL_LEVELS), ((0, 64),), -0.2, 0.2)), 0.05, 0.4)
    observed = centred(keys[3], (GRID_ROWS, NXP, SLOTS), 1.0, 6.0, ((0, 256), (1, 2)), jnp.float32)
    slot_error_variance = jnp.clip(jnp.exp(math.log(4.0) - 2.7725887 * jax.random.uniform(keys[4], (GRID_ROWS, NXP, SLOTS), jnp.float32) ** shard_levels(keys[4], (GRID_ROWS, NXP, SLOTS), ((0, 256), (1, 2)), -0.2, 0.2)), 0.25, 4.0)
    sensor_target_site = with_ends(jax.random.randint(keys[5], (GRID_ROWS, NXP, SLOTS), 0, VERTICAL_LEVELS * PATCH), jax.random.fold_in(keys[5], 1), 0, (VERTICAL_LEVELS * PATCH) - 1).astype(jnp.int32)
    patch_live_count = draw_patch_live_count(jax.random.fold_in(keys[7], 71), 0)
    return dict(starting_concentration_per_run=starting_concentration_per_run, diffusivity=diffusivity, run_layer_stability_number=run_layer_stability_number, observed=observed, slot_error_variance=slot_error_variance, sensor_target_site=sensor_target_site, patch_live_count=patch_live_count)


HIGHEST = lax.Precision.HIGHEST

def advance(padded, diffusivity, member_wind):
    centre = padded[..., 1:-1, 1:-1]
    northern = padded[..., :-2, 1:-1]
    southern = padded[..., 2:, 1:-1]
    western = padded[..., 1:-1, :-2]
    easterly_side = padded[..., 1:-1, 2:]
    spread = northern + southern + (western + easterly_side) - 4.0 * centre
    return centre + diffusivity * spread - member_wind * (centre - western)

def analyse(background, sampled, observed, slot_error_variance, patch_live_count):
    members = background.shape[1]
    slots = observed.shape[-1]
    centre_mean = lax.optimization_barrier(jnp.mean(background, axis=1, keepdims=True))
    perturbed = background - centre_mean
    sampled_mean = lax.optimization_barrier(jnp.mean(sampled, axis=1, keepdims=True))
    sampled_pert = sampled - sampled_mean
    live_slot = jnp.arange(slots)[None, :] < patch_live_count[:, None]
    precision_obs = jnp.where(live_slot, 1.0 / slot_error_variance, 0.0 * slot_error_variance)
    innovation = observed - sampled_mean[:, 0, :]
    weighted = sampled_pert * precision_obs[:, None, :]
    identity = jnp.eye(members, dtype=background.dtype)
    system = jnp.einsum('pms,pns->pmn', weighted, sampled_pert, precision=HIGHEST) + (members - 1.0) * identity
    source_term = jnp.einsum('pms,ps->pm', weighted, innovation, precision=HIGHEST)
    factor = jnp.linalg.cholesky(system)
    halfway = lax.linalg.triangular_solve(factor, source_term[:, :, None], left_side=True, lower=True)
    mean_weight = lax.linalg.triangular_solve(factor, halfway, left_side=True, lower=True, transpose_a=True)[:, :, 0]
    norm_scale = jnp.sqrt(lax.optimization_barrier(jnp.sum(system * system, axis=(1, 2))))
    iterate = system / norm_scale[:, None, None]
    inverse_root = jnp.broadcast_to(identity, system.shape)
    for sweep in range(NS_ITERS):
        update = 1.5 * identity - 0.5 * jnp.einsum('pij,pjk->pik', inverse_root, iterate, precision=HIGHEST)
        iterate = jnp.einsum('pij,pjk->pik', iterate, update, precision=HIGHEST)
        inverse_root = jnp.einsum('pij,pjk->pik', update, inverse_root, precision=HIGHEST)
    spread_weight = inverse_root * jnp.sqrt((members - 1.0) / norm_scale)[:, None, None]
    combined = spread_weight + mean_weight[:, :, None]
    return centre_mean + jnp.einsum('pki,pkc->pic', combined, perturbed, precision=HIGHEST)

def reference(starting_concentration_per_run, diffusivity, run_layer_stability_number, observed, slot_error_variance, sensor_target_site, patch_live_count):

    def march_single_run(inputs):
        member_state, member_wind = inputs
        for stepno in range(STEPS):
            padded = jnp.pad(member_state, ((0, 0), (1, 1), (1, 1)))
            member_state = advance(padded, diffusivity, member_wind[:, None, None])
        return member_state
    predicted_concentration = lax.map(march_single_run, (starting_concentration_per_run, run_layer_stability_number))
    line_by_line = jnp.transpose(predicted_concentration, (2, 0, 1, 3))

    def analyse_row(inputs):
        row_state, row_observed, row_variance, row_cell, row_count = inputs
        members, levels, row_width = row_state.shape
        patches = row_width // PATCH
        background = jnp.transpose(row_state.reshape(members, levels, patches, PATCH), (2, 0, 1, 3)).reshape(patches, members, levels * PATCH)
        cell_index = jnp.broadcast_to(row_cell[:, None, :], (patches, members, row_cell.shape[-1]))
        sampled = jnp.take_along_axis(background, cell_index, axis=2)
        result = analyse(background, sampled, row_observed, row_variance, row_count)
        return jnp.transpose(result.reshape(patches, members, levels, PATCH), (1, 2, 0, 3)).reshape(members, levels, row_width)
    analysed = lax.map(analyse_row, (line_by_line, observed, slot_error_variance, sensor_target_site, patch_live_count))
    return jnp.transpose(analysed, (1, 2, 0, 3))
```

```python
import jax
import jax.numpy as jnp
from jax import lax
from jax.experimental import pallas as pl
from jax.experimental.pallas import tpu as pltpu
from jax.sharding import Mesh
from jax.sharding import PartitionSpec as P

LEVELS = 8
PATCH = 128
STEPS = 4
NS_ITERS = 4
MEMBERS = 64
ROWS = 64
COLS = 256
TALL = ROWS + 2 * STEPS
GRP = ("grp_0", "grp_1")
SUB_GRP = ("sub", "grp_0", "grp_1")
HIGHEST = lax.Precision.HIGHEST
VMEM_LIMIT = 24 * 1024 * 1024


def pack_kernel(rep_ref, x_ref, d_ref, first_ref, last_ref, side_ref):
    for h in range(2):
        cols = slice(h * PATCH, (h + 1) * PATCH)
        for l in range(LEVELS):
            top = x_ref[ROWS * l : ROWS * l + 8, cols]
            end = x_ref[ROWS * l + ROWS - 8 : ROWS * l + ROWS, cols]
            first_ref[pl.ds(8 * h + l, STEPS, stride=16), :] = top[:STEPS]
            last_ref[pl.ds(8 * h + l, STEPS, stride=16), :] = end[8 - STEPS :]
        first_ref[64 + 8 * h : 72 + 8 * h, :] = d_ref[0:8, cols]
        last_ref[64 + 8 * h : 72 + 8 * h, :] = d_ref[ROWS - 8 : ROWS, cols]
    half = pl.ds(pl.multiple_of((1 - rep_ref[0]) * PATCH, PATCH), PATCH)
    side_ref[0 : LEVELS * ROWS, :] = x_ref[:, half]
    side_ref[LEVELS * ROWS :, :] = d_ref[:, half]


def forecast_kernel(rep_ref, x_ref, d_ref, below_ref, above_ref, side_ref, corner_ref, wind_ref, out_ref, a_ref, b_ref, w_ref):
    rep = rep_ref[0]
    lane = lax.broadcasted_iota(jnp.int32, (8, PATCH), 1)
    low = jnp.where(rep == 0, 0, PATCH - STEPS)
    keep = (lane >= low) & (lane < low + STEPS)
    keep_rows = jnp.broadcast_to(keep[:1], (ROWS, PATCH))
    for l in range(LEVELS):
        for t in range(2):
            a_ref[pl.ds(24 * STEPS + 8 * t + l, ROWS, stride=24), :] = x_ref[
                ROWS * l : ROWS * (l + 1), t * PATCH : (t + 1) * PATCH
            ]
        a_ref[pl.ds(24 * STEPS + 16 + l, ROWS, stride=24), :] = jnp.where(
            keep_rows, side_ref[ROWS * l : ROWS * (l + 1), :], 0.0
        )
    for ref, base, corner in ((above_ref, 0, 40), (below_ref, STEPS + ROWS, 0)):
        for r in range(STEPS):
            at = 24 * (base + r)
            a_ref[at : at + 16, :] = ref[16 * r : 16 * r + 16, :]
            a_ref[at + 16 : at + 24, :] = jnp.where(
                keep, corner_ref[corner + 8 * r : corner + 8 * r + 8, :], 0.0
            )
    for t in range(2):
        w_ref[80 * t + 8 : 80 * t + 8 + ROWS, :] = d_ref[:, t * PATCH : (t + 1) * PATCH]
    w_ref[168 : 168 + ROWS, :] = jnp.where(keep_rows, side_ref[LEVELS * ROWS :, :], 0.0)
    for ref, base, corner in ((above_ref, 0, 72), (below_ref, 8 + ROWS, 32)):
        for t in range(2):
            w_ref[80 * t + base : 80 * t + base + 8, :] = ref[64 + 8 * t : 72 + 8 * t, :]
        w_ref[160 + base : 168 + base, :] = jnp.where(keep, corner_ref[corner : corner + 8, :], 0.0)
    wind = wind_ref[...]
    winds = [wind, wind, jnp.where(keep, wind, 0.0)]
    first_lane, last_lane = lane == 0, lane == PATCH - 1

    def tiles(ref, row):
        return [ref[pl.ds(pl.multiple_of(24 * row + 8 * t, 8), 8), :] for t in range(3)]

    for step in range(STEPS):
        src, dst = (a_ref, b_ref) if step % 2 == 0 else (b_ref, a_ref)

        def body(row, carry, src=src, dst=dst, step=step):
            northern, centre = carry
            southern = tiles(src, row + 1)
            right = [pltpu.roll(v, 1, 1) for v in centre]
            left = [pltpu.roll(v, PATCH - 1, 1) for v in centre]
            for t in range(3 if step < STEPS - 1 else 2):
                west = jnp.where(first_lane, right[(t + 2) % 3], right[t])
                east = jnp.where(last_lane, left[(t + 1) % 3], left[t])
                spread = northern[t] + southern[t] + (west + east) - 4.0 * centre[t]
                d_row = w_ref[pl.ds(80 * t + row + STEPS, 1), :]
                new = centre[t] + d_row * spread - winds[t] * (centre[t] - west)
                if step < STEPS - 1:
                    dst[pl.ds(pl.multiple_of(24 * row + 8 * t, 8), 8), :] = new
                else:
                    at = pl.multiple_of(16 * (row - STEPS) + 8 * t, 8)
                    out_ref[pl.ds(at, 8), :] = new
            return centre, southern

        first = step + 1
        lax.fori_loop(
            first, TALL - first, body, (tiles(src, first - 1), tiles(src, first)), unroll=2
        )


def analysis_kernel(count_ref, x_ref, obs_ref, var_ref, site_ref, out_ref, pert_ref):
    members = MEMBERS
    lanes = lax.broadcasted_iota(jnp.int32, (8, PATCH), 1)
    site = site_ref[...]
    level = site // PATCH
    column = site - level * PATCH
    means = [[None] * LEVELS for _ in range(2)]
    sampled = []
    for p in range(2):
        pick = jnp.broadcast_to(column[p : p + 1, :], (members, PATCH))
        got = jnp.zeros((members, PATCH), jnp.float32)
        for l in range(LEVELS):
            block = x_ref[pl.ds(8 * p + l, members, stride=16), :]
            mean = jnp.sum(block, axis=0, keepdims=True) * (1.0 / members)
            means[p][l] = mean
            pert_ref[p * members : (p + 1) * members, l * PATCH : (l + 1) * PATCH] = block - mean
            here = jnp.take_along_axis(block, pick, axis=1, mode="promise_in_bounds")
            got = jnp.where(level[p : p + 1, :] == l, here, got)
        sampled.append(got)
    perts, weighteds, forcings = [], [], []
    for p in range(2):
        got = sampled[p]
        mean = jnp.sum(got, axis=0, keepdims=True) * (1.0 / members)
        pert = got - mean
        live = lanes[:1] < count_ref[p]
        precision = jnp.where(live, 1.0 / var_ref[p : p + 1, :], 0.0)
        weighted = pert * precision
        innovation = obs_ref[p : p + 1, :] - mean
        perts.append(pert)
        weighteds.append(weighted)
        forcings.append(jnp.sum(weighted * innovation, axis=1, keepdims=True))
    nt = (((1,), (1,)), ((), ()))
    both = 2 * members
    cross = lax.dot_general(
        jnp.concatenate(weighteds, 0), jnp.concatenate(perts, 0), nt,
        precision=HIGHEST, preferred_element_type=jnp.float32,
    )
    row_id = lax.broadcasted_iota(jnp.int32, (both, both), 0)
    col_id = lax.broadcasted_iota(jnp.int32, (both, both), 1)
    eye = (row_id == col_id).astype(jnp.float32)
    system = jnp.where((row_id < members) == (col_id < members), cross, 0.0) + (members - 1.0) * eye

    m = system[:members, :] + system[members:, :]
    left = lanes < members
    m = [m[8 * q : 8 * q + 8, :] for q in range(8)]
    f = [
        jnp.where(left, forcings[0][8 * q : 8 * q + 8, :], forcings[1][8 * q : 8 * q + 8, :])
        for q in range(8)
    ]
    sub_id = lax.broadcasted_iota(jnp.int32, (8, PATCH), 0)
    inverse = [jnp.zeros((8, PATCH), jnp.float32) for _ in range(8)]
    for k in range(members):
        kq, kr = divmod(k, 8)
        at = jnp.where(left, k, members + k)
        column_k = [jnp.take_along_axis(v, at, axis=1, mode="promise_in_bounds") for v in m]
        inv = 1.0 / column_k[kq][kr : kr + 1, :]
        row_k = m[kq][kr : kr + 1, :] * inv
        f_k = f[kq][kr : kr + 1, :] * inv
        here = sub_id == kr
        inverse[kq] = jnp.where(here, inv, inverse[kq])
        column_k[kq] = jnp.where(here, 0.0, column_k[kq])
        m = [v - c * row_k for v, c in zip(m, column_k)]
        f = [v - c * f_k for v, c in zip(f, column_k)]
    weight = jnp.concatenate([v * i for v, i in zip(f, inverse)], 0)

    squares = jnp.sum(system * system, axis=1, keepdims=True)
    norms = [
        jnp.sqrt(jnp.sum(squares[p * members : (p + 1) * members], axis=0, keepdims=True))
        for p in range(2)
    ]
    norm = jnp.where(row_id[:, :1] < members, norms[0], norms[1])

    def mm(a, b):
        return jnp.dot(a, b, precision=HIGHEST, preferred_element_type=jnp.float32)

    iterate = system / norm
    root = None
    for sweep in range(NS_ITERS):
        update = 1.5 * eye - 0.5 * (iterate if root is None else mm(root, iterate))
        if sweep < NS_ITERS - 1:
            iterate = mm(iterate, update)
        root = update if root is None else mm(update, root)
    spread = root * jnp.sqrt((members - 1.0) / norm)
    zero = jnp.zeros((members, PATCH), jnp.float32)
    left_all = col_id[:members] < members
    combined = spread + jnp.concatenate(
        [jnp.where(left_all, weight, zero), jnp.where(left_all, zero, weight)], 0
    )
    tn = (((0,), (0,)), ((), ()))
    for l in range(LEVELS):
        moved = lax.dot_general(
            combined, pert_ref[:, l * PATCH : (l + 1) * PATCH], tn,
            precision=HIGHEST, preferred_element_type=jnp.float32,
        )
        for p in range(2):
            out_ref[pl.ds(8 * p + l, members, stride=16), :] = (
                moved[p * members : (p + 1) * members] + means[p][l]
            )


def unpack_kernel(x_ref, out_ref):
    for l in range(LEVELS):
        for h in range(2):
            out_ref[ROWS * l : ROWS * (l + 1), h * PATCH : (h + 1) * PATCH] = x_ref[
                pl.ds(8 * h + l, ROWS, stride=16), :
            ]


VMEM = pl.BlockSpec(memory_space=pltpu.VMEM)
SMEM = pl.BlockSpec(memory_space=pltpu.SMEM)


def call(kernel, outs, specs, scratch=(), flops=1_000_000, name=None):
    shapes = [jax.ShapeDtypeStruct(s, jnp.float32) for s in outs]
    return pl.pallas_call(
        kernel,
        out_shape=shapes if len(shapes) > 1 else shapes[0],
        in_specs=specs,
        out_specs=[VMEM] * len(shapes) if len(shapes) > 1 else VMEM,
        scratch_shapes=[pltpu.VMEM(s, jnp.float32) for s in scratch],
        compiler_params=pltpu.CompilerParams(vmem_limit_bytes=VMEM_LIMIT),
        cost_estimate=pl.CostEstimate(flops=flops, bytes_accessed=1_000_000, transcendentals=0),
        name=name,
    )


def on_device(start, diffusivity, stability, observed, variance, site, live):
    rep = lax.axis_index("rep").astype(jnp.int32).reshape(1)
    x = start.reshape(LEVELS * ROWS, COLS)
    first, last, side = call(
        pack_kernel,
        [(80, PATCH), (80, PATCH), ((LEVELS + 1) * ROWS, PATCH)],
        [SMEM, VMEM, VMEM],
        name="pack",
    )(rep, x, diffusivity)
    n = lax.axis_size("sub")
    below = lax.ppermute(first, "sub", [(i + 1, i) for i in range(n - 1)])
    above = lax.ppermute(last, "sub", [(i, i + 1) for i in range(n - 1)])
    swap = [(0, 1), (1, 0)]
    side = lax.ppermute(side, "rep", swap)
    ends = jnp.concatenate([below, above], axis=0).reshape(10, 2, 8, PATCH)
    corner = lax.dynamic_index_in_dim(ends, 1 - rep[0], axis=1, keepdims=False)
    corner = lax.ppermute(corner.reshape(80, PATCH), "rep", swap)
    wind = jnp.broadcast_to(stability.reshape(LEVELS, 1), (LEVELS, PATCH))
    forecast = call(
        forecast_kernel,
        [(ROWS * 16, PATCH)],
        [SMEM] + [VMEM] * 7,
        scratch=[(TALL * 24, PATCH), (TALL * 24, PATCH), (3 * (ROWS + 16), PATCH)],
        name="forecast",
    )(rep, x, diffusivity, below, above, side, corner, wind)
    gathered = lax.all_to_all(forecast.reshape(ROWS, 16, PATCH), GRP, 0, 0, tiled=True)
    analysed = call(
        analysis_kernel,
        [(MEMBERS * 16, PATCH)],
        [SMEM] + [VMEM] * 4,
        scratch=[(2 * MEMBERS, LEVELS * PATCH)],
        name="analysis",
    )(
        live.reshape(2),
        gathered.reshape(MEMBERS * 16, PATCH),
        observed.reshape(2, PATCH),
        variance.reshape(2, PATCH),
        site.reshape(2, PATCH),
    )
    returned = lax.all_to_all(analysed.reshape(MEMBERS, 16, PATCH), GRP, 0, 0, tiled=True)
    out = call(unpack_kernel, [(LEVELS * ROWS, COLS)], [VMEM], name="unpack")(
        returned.reshape(ROWS * 16, PATCH)
    )
    return out.reshape(1, LEVELS, ROWS, COLS)


def solution(mesh):
    split = Mesh(
        mesh.devices.reshape(16, 4, mesh.shape["sub"], mesh.shape["rep"]),
        ("grp_0", "grp_1", "sub", "rep"),
    )
    return jax.shard_map(
        on_device,
        mesh=split,
        in_specs=(
            P(GRP, None, "sub", "rep"),
            P("sub", "rep"),
            P(GRP, None),
            P(SUB_GRP, "rep", None),
            P(SUB_GRP, "rep", None),
            P(SUB_GRP, "rep", None),
            P(SUB_GRP, "rep"),
        ),
        out_specs=P(GRP, None, "sub", "rep"),
        check_vma=False,
    )
```

```python
import jax
import jax.numpy as jnp
from jax import lax
from jax.experimental import pallas as pl
from jax.experimental.pallas import tpu as pltpu
from jax.sharding import Mesh
from jax.sharding import PartitionSpec as P

LEVELS = 8
PATCH = 128
STEPS = 4
NS_ITERS = 4
MEMBERS = 64
ROWS = 64
COLS = 256
TALL = ROWS + 2 * STEPS
GRP = ("grp_0", "grp_1")
SUB_GRP = ("sub", "grp_0", "grp_1")
HIGHEST = lax.Precision.HIGHEST
VMEM_LIMIT = 24 * 1024 * 1024


def pack_kernel(rep_ref, x_ref, d_ref, first_ref, last_ref, side_ref, top_ref, end_ref, dtop_ref, dend_ref, sems):
    half = pl.ds(pl.multiple_of((1 - rep_ref[0]) * PATCH, PATCH), PATCH)
    copies = [
        pltpu.make_async_copy(src, dst, sems.at[i])
        for i, (src, dst) in enumerate(
            (
                (x_ref.at[:, pl.ds(0, 8), :], top_ref),
                (x_ref.at[:, pl.ds(ROWS - 8, 8), :], end_ref),
                (d_ref.at[pl.ds(0, 8), :], dtop_ref),
                (d_ref.at[pl.ds(ROWS - 8, 8), :], dend_ref),
                (x_ref.at[:, :, half], side_ref.at[pl.ds(0, LEVELS)]),
                (d_ref.at[:, half], side_ref.at[LEVELS]),
            )
        )
    ]
    for copy in copies:
        copy.start()
    for copy in copies[:4]:
        copy.wait()
    for h in range(2):
        cols = slice(h * PATCH, (h + 1) * PATCH)
        for l in range(LEVELS):
            first_ref[pl.ds(8 * h + l, STEPS, stride=16), :] = top_ref[l, :STEPS, cols]
            last_ref[pl.ds(8 * h + l, STEPS, stride=16), :] = end_ref[l, 8 - STEPS :, cols]
        first_ref[64 + 8 * h : 72 + 8 * h, :] = dtop_ref[:, cols]
        last_ref[64 + 8 * h : 72 + 8 * h, :] = dend_ref[:, cols]
    for copy in copies[4:]:
        copy.wait()


def forecast_kernel(
    rep_ref, count_ref, x_ref, d_ref, below_ref, above_ref, side_ref, corner_ref, wind_ref, obs_hbm, var_hbm, site_hbm,
    out_ref, obs_out, precision_out, site_out, a_ref, b_ref, w_ref, var_ref, sems,
):
    copies = [
        pltpu.make_async_copy(src, dst, sems.at[i])
        for i, (src, dst) in enumerate(
            ((obs_hbm, obs_out), (var_hbm, var_ref), (site_hbm, site_out))
        )
    ]
    for copy in copies:
        copy.start()
    rep = rep_ref[0]
    lane = lax.broadcasted_iota(jnp.int32, (8, PATCH), 1)
    low = jnp.where(rep == 0, 0, PATCH - STEPS)
    keep = (lane >= low) & (lane < low + STEPS)
    keep_rows = jnp.broadcast_to(keep[:1], (ROWS, PATCH))
    zero = jnp.zeros((8, PATCH), jnp.float32)
    own = 24 * (STEPS + 1)
    for l in range(LEVELS):
        for t in range(2):
            a_ref[pl.ds(own + 8 * t + l, ROWS, stride=24), :] = x_ref[
                ROWS * l : ROWS * (l + 1), t * PATCH : (t + 1) * PATCH
            ]
        a_ref[pl.ds(own + 16 + l, ROWS, stride=24), :] = jnp.where(
            keep_rows, side_ref[ROWS * l : ROWS * (l + 1), :], 0.0
        )
    for ref, base, corner in ((above_ref, 1, 40), (below_ref, 1 + STEPS + ROWS, 0)):
        for r in range(STEPS):
            at = 24 * (base + r)
            a_ref[at : at + 16, :] = ref[16 * r : 16 * r + 16, :]
            a_ref[at + 16 : at + 24, :] = jnp.where(
                keep, corner_ref[corner + 8 * r : corner + 8 * r + 8, :], 0.0
            )
    for ref in (a_ref, b_ref):
        for at in (0, 24 * (TALL + 1)):
            for t in range(3):
                ref[at + 8 * t : at + 8 * t + 8, :] = zero
    for t in range(2):
        w_ref[80 * t + 8 : 80 * t + 8 + ROWS, :] = d_ref[:, t * PATCH : (t + 1) * PATCH]
    w_ref[168 : 168 + ROWS, :] = jnp.where(keep_rows, side_ref[LEVELS * ROWS :, :], 0.0)
    for ref, base, corner in ((above_ref, 0, 72), (below_ref, 8 + ROWS, 32)):
        for t in range(2):
            w_ref[80 * t + base : 80 * t + base + 8, :] = ref[64 + 8 * t : 72 + 8 * t, :]
        w_ref[160 + base : 168 + base, :] = jnp.where(keep, corner_ref[corner : corner + 8, :], 0.0)
    wind = wind_ref[...]
    winds = [wind, wind, jnp.where(keep, wind, 0.0)]
    first_lane, last_lane = lane == 0, lane == PATCH - 1

    for step in range(STEPS):
        src, dst = (a_ref, b_ref) if step % 2 == 0 else (b_ref, a_ref)
        final = step == STEPS - 1
        skip = STEPS if final else 0

        def body(block, carry, src=src, dst=dst, final=final, skip=skip):
            top = pl.multiple_of(24 * (8 * block + skip), 8)

            def tiles(row):
                return [src[pl.ds(top + 24 * row + 8 * t, 8), :] for t in range(3)]

            northern, centre = tiles(0), tiles(1)
            for row in range(8):
                southern = tiles(row + 2)
                right = [pltpu.roll(v, 1, 1) for v in centre]
                left = [pltpu.roll(v, PATCH - 1, 1) for v in centre]
                for t in range(2 if final else 3):
                    west = jnp.where(first_lane, right[(t + 2) % 3], right[t])
                    east = jnp.where(last_lane, left[(t + 1) % 3], left[t])
                    spread = northern[t] + southern[t] + (west + east) - 4.0 * centre[t]
                    d_row = w_ref[pl.ds(80 * t + 8 * block + skip + row + STEPS, 1), :]
                    new = centre[t] + d_row * spread - winds[t] * (centre[t] - west)
                    if final:
                        at = pl.multiple_of(16 * 8 * block, 8) + 16 * row + 8 * t
                        out_ref[pl.ds(at, 8), :] = new
                    else:
                        dst[pl.ds(top + 24 * (row + 1) + 8 * t, 8), :] = new
                northern, centre = centre, southern
            return carry

        lax.fori_loop(0, (TALL - 2 * skip) // 8, body, 0)

    for copy in copies:
        copy.wait()
    for p in range(2):
        live = lane[:1] < count_ref[p]
        precision_out[p : p + 1, :] = jnp.where(live, 1.0 / var_ref[p : p + 1, :], 0.0)


def analysis_kernel(x_ref, obs_ref, precision_ref, site_ref, out_ref, pert_ref):
    members = MEMBERS
    both = 2 * members
    lanes = lax.broadcasted_iota(jnp.int32, (8, PATCH), 1)
    site = site_ref[...]
    level = site // PATCH
    column = site - level * PATCH
    means = [[None] * LEVELS for _ in range(2)]
    perts, weighteds, forcings = [], [], []
    for p in range(2):
        pick = jnp.broadcast_to(column[p : p + 1, :], (members, PATCH))
        got = jnp.zeros((members, PATCH), jnp.float32)
        for l in range(LEVELS):
            block = x_ref[pl.ds(8 * p + l, members, stride=16), :]
            mean = jnp.sum(block, axis=0, keepdims=True) * (1.0 / members)
            means[p][l] = mean
            pert_ref[p * members : (p + 1) * members, l * PATCH : (l + 1) * PATCH] = block - mean
            here = jnp.take_along_axis(block, pick, axis=1, mode="promise_in_bounds")
            got = jnp.where(level[p : p + 1, :] == l, here, got)
        mean = jnp.sum(got, axis=0, keepdims=True) * (1.0 / members)
        pert = got - mean
        weighted = pert * precision_ref[p : p + 1, :]
        perts.append(pert)
        weighteds.append(weighted)
        innovation = obs_ref[p : p + 1, :] - mean
        forcings.append(jnp.sum(weighted * innovation, axis=1, keepdims=True))
    nt = (((1,), (1,)), ((), ()))
    cross = lax.dot_general(
        jnp.concatenate(weighteds, 0), jnp.concatenate(perts, 0), nt,
        precision=HIGHEST, preferred_element_type=jnp.float32,
    )
    row_id = lax.broadcasted_iota(jnp.int32, (both, both), 0)
    col_id = lax.broadcasted_iota(jnp.int32, (both, both), 1)
    eye = (row_id == col_id).astype(jnp.float32)
    system = jnp.where((row_id < members) == (col_id < members), cross, 0.0) + (members - 1.0) * eye
    moved = []

    def spread_steps():
        def mm(a, b):
            return jnp.dot(a, b, precision=HIGHEST, preferred_element_type=jnp.float32)

        squares = jnp.sum(system * system, axis=1, keepdims=True)
        norms = [
            jnp.sqrt(jnp.sum(squares[p * members : (p + 1) * members], axis=0, keepdims=True))
            for p in range(2)
        ]
        norm = jnp.where(row_id[:, :1] < members, norms[0], norms[1])
        iterate = system / norm
        root = update = 1.5 * eye - 0.5 * iterate
        for sweep in range(1, NS_ITERS):
            iterate = mm(iterate, update)
            yield
            update = 1.5 * eye - 0.5 * mm(root, iterate)
            yield
            root = mm(update, root)
            yield
        spread = root * jnp.sqrt((members - 1.0) / norm)
        tn = (((0,), (0,)), ((), ()))
        for l in range(LEVELS):
            moved.append(
                lax.dot_general(
                    spread, pert_ref[:, l * PATCH : (l + 1) * PATCH], tn,
                    precision=HIGHEST, preferred_element_type=jnp.float32,
                )
            )
            yield

    m = system[:members, :] + system[members:, :]
    left = lanes < members
    m = [m[8 * q : 8 * q + 8, :] for q in range(8)]
    f = [
        jnp.where(left, forcings[0][8 * q : 8 * q + 8, :], forcings[1][8 * q : 8 * q + 8, :])
        for q in range(8)
    ]
    sub_id = lax.broadcasted_iota(jnp.int32, (8, PATCH), 0)
    even = sub_id % 2 == 0
    same = [None] * 8
    other = [None] * 8
    steps = spread_steps()
    for k in range(0, members, 2):
        next(steps, None)
        q, r = divmod(k, 8)
        c0, c1 = (
            [jnp.take_along_axis(v, jnp.where(left, j, members + j), axis=1, mode="promise_in_bounds") for v in m]
            for j in (k, k + 1)
        )
        a, b, d = c0[q][r : r + 1, :], c0[q][r + 1 : r + 2, :], c1[q][r + 1 : r + 2, :]
        inv = 1.0 / (a * d - b * b)
        a, b, d = a * inv, b * inv, d * inv
        pair = (sub_id // 2) * 2 == r
        keep_same, keep_other = jnp.where(even, d, a), jnp.broadcast_to(-b, (8, PATCH))
        same[q] = keep_same if r == 0 else jnp.where(pair, keep_same, same[q])
        other[q] = keep_other if r == 0 else jnp.where(pair, keep_other, other[q])
        r0, r1 = m[q][r : r + 1, :], m[q][r + 1 : r + 2, :]
        f0, f1 = f[q][r : r + 1, :], f[q][r + 1 : r + 2, :]
        c0[q], c1[q] = jnp.where(pair, 0.0, c0[q]), jnp.where(pair, 0.0, c1[q])
        r0, r1 = d * r0 - b * r1, a * r1 - b * r0
        f0, f1 = d * f0 - b * f1, a * f1 - b * f0
        m = [v - (u * r0 + w * r1) for v, u, w in zip(m, c0, c1)]
        f = [v - (u * f0 + w * f1) for v, u, w in zip(f, c0, c1)]
    for _ in steps:
        pass
    weight = []
    for q in range(8):
        partner = jnp.where(even, pltpu.roll(f[q], 7, 0), pltpu.roll(f[q], 1, 0))
        weight.append(same[q] * f[q] + other[q] * partner)
    weight = jnp.concatenate(weight, 0)
    turned = pltpu.roll(weight, members, 1)
    left_all = col_id[:members] < members
    for p in range(2):
        wide = jnp.where(left_all, weight, turned) if p == 0 else jnp.where(left_all, turned, weight)
        for l in range(LEVELS):
            rows = slice(p * members, (p + 1) * members)
            shift = jnp.sum(wide * pert_ref[rows, l * PATCH : (l + 1) * PATCH], axis=0, keepdims=True)
            out_ref[pl.ds(8 * p + l, members, stride=16), :] = moved[l][rows] + (means[p][l] + shift)


def unpack_kernel(x_ref, out_ref):
    for l in range(LEVELS):
        for h in range(2):
            out_ref[ROWS * l : ROWS * (l + 1), h * PATCH : (h + 1) * PATCH] = x_ref[
                pl.ds(8 * h + l, ROWS, stride=16), :
            ]


VMEM = pl.BlockSpec(memory_space=pltpu.VMEM)
SMEM = pl.BlockSpec(memory_space=pltpu.SMEM)
HBM = pl.BlockSpec(memory_space=pltpu.HBM)


def f32(*dims):
    return jax.ShapeDtypeStruct(dims, jnp.float32)


def call(kernel, outs, specs, scratch=(), flops=1_000_000, name=None):
    return pl.pallas_call(
        kernel,
        out_shape=outs if len(outs) > 1 else outs[0],
        in_specs=specs,
        out_specs=[VMEM] * len(outs) if len(outs) > 1 else VMEM,
        scratch_shapes=scratch,
        compiler_params=pltpu.CompilerParams(vmem_limit_bytes=VMEM_LIMIT),
        cost_estimate=pl.CostEstimate(flops=flops, bytes_accessed=1_000_000, transcendentals=0),
        name=name,
    )


def on_device(start, diffusivity, stability, observed, variance, site, live):
    rep = lax.axis_index("rep").astype(jnp.int32).reshape(1)
    first, last, side = call(
        pack_kernel,
        [f32(80, PATCH), f32(80, PATCH), f32(LEVELS + 1, ROWS, PATCH)],
        [SMEM, HBM, HBM],
        scratch=[
            pltpu.VMEM((LEVELS, 8, COLS), jnp.float32),
            pltpu.VMEM((LEVELS, 8, COLS), jnp.float32),
            pltpu.VMEM((8, COLS), jnp.float32),
            pltpu.VMEM((8, COLS), jnp.float32),
            pltpu.SemaphoreType.DMA((6,)),
        ],
        name="pack",
    )(rep, start.reshape(LEVELS, ROWS, COLS), diffusivity)
    n = lax.axis_size("sub")
    below = lax.ppermute(first, "sub", [(i + 1, i) for i in range(n - 1)])
    above = lax.ppermute(last, "sub", [(i, i + 1) for i in range(n - 1)])
    swap = [(0, 1), (1, 0)]
    side = lax.ppermute(side, "rep", swap)
    ends = jnp.concatenate([below, above], axis=0).reshape(10, 2, 8, PATCH)
    corner = lax.dynamic_index_in_dim(ends, 1 - rep[0], axis=1, keepdims=False)
    corner = lax.ppermute(corner.reshape(80, PATCH), "rep", swap)
    wind = jnp.broadcast_to(stability.reshape(LEVELS, 1), (LEVELS, PATCH))
    state = pltpu.VMEM((24 * (TALL + 2), PATCH), jnp.float32)
    forecast, obs, precision, cell = call(
        forecast_kernel,
        [f32(ROWS * 16, PATCH), f32(2, PATCH), f32(2, PATCH), jax.ShapeDtypeStruct((2, PATCH), jnp.int32)],
        [SMEM] * 2 + [VMEM] * 7 + [HBM] * 3,
        scratch=[
            state,
            state,
            pltpu.VMEM((3 * (ROWS + 16), PATCH), jnp.float32),
            pltpu.VMEM((2, PATCH), jnp.float32),
            pltpu.SemaphoreType.DMA((3,)),
        ],
        name="forecast",
    )(
        rep,
        live.reshape(2),
        start.reshape(LEVELS * ROWS, COLS),
        diffusivity,
        below,
        above,
        side.reshape((LEVELS + 1) * ROWS, PATCH),
        corner,
        wind,
        observed.reshape(2, PATCH),
        variance.reshape(2, PATCH),
        site.reshape(2, PATCH),
    )
    gathered = lax.all_to_all(forecast.reshape(ROWS, 16, PATCH), GRP, 0, 0, tiled=True)
    analysed = call(
        analysis_kernel,
        [f32(MEMBERS * 16, PATCH)],
        [VMEM] * 4,
        scratch=[pltpu.VMEM((2 * MEMBERS, LEVELS * PATCH), jnp.float32)],
        name="analysis",
    )(gathered.reshape(MEMBERS * 16, PATCH), obs, precision, cell)
    returned = lax.all_to_all(analysed.reshape(MEMBERS, 16, PATCH), GRP, 0, 0, tiled=True)
    out = call(unpack_kernel, [f32(LEVELS * ROWS, COLS)], [VMEM], name="unpack")(
        returned.reshape(ROWS * 16, PATCH)
    )
    return out.reshape(1, LEVELS, ROWS, COLS)


def solution(mesh):
    split = Mesh(
        mesh.devices.reshape(16, 4, mesh.shape["sub"], mesh.shape["rep"]),
        ("grp_0", "grp_1", "sub", "rep"),
    )
    return jax.shard_map(
        on_device,
        mesh=split,
        in_specs=(
            P(GRP, None, "sub", "rep"),
            P("sub", "rep"),
            P(GRP, None),
            P(SUB_GRP, "rep", None),
            P(SUB_GRP, "rep", None),
            P(SUB_GRP, "rep", None),
            P(SUB_GRP, "rep"),
        ),
        out_specs=P(GRP, None, "sub", "rep"),
        check_vma=False,
    )
```

```python
import jax
import jax.numpy as jnp
from jax import lax
from jax.experimental import pallas as pl
from jax.experimental.pallas import tpu as pltpu
from jax.sharding import Mesh
from jax.sharding import PartitionSpec as P

LEVELS = 8
PATCH = 128
STEPS = 4
NS_ITERS = 4
MEMBERS = 64
ROWS = 64
COLS = 256
TALL = ROWS + 2 * STEPS
GRP = ("grp_0", "grp_1")
SUB_GRP = ("sub", "grp_0", "grp_1")
HIGHEST = lax.Precision.HIGHEST
VMEM_LIMIT = 24 * 1024 * 1024
PACK_LIMIT = 56 * 1024 * 1024
SUBS = 4
BLOCK = 72


def pack_kernel(
    x_ref, d_ref, stability_ref, obs_hbm, var_hbm, site_hbm, count_hbm, send_ref,
    top_ref, end_ref, dtop_ref, dend_ref, edge_ref, dedge_ref, calm_ref, obs_ref, var_ref, site_ref, count_ref, sems,
):
    y, rep = lax.axis_index("sub"), lax.axis_index("rep")
    half = pl.ds(pl.multiple_of((1 - rep) * PATCH, PATCH), PATCH)
    copies = [
        pltpu.make_async_copy(src, dst, sems.at[i])
        for i, (src, dst) in enumerate(
            (
                (x_ref.at[:, :, half], edge_ref),
                (d_ref.at[:, half], dedge_ref),
                (x_ref.at[:, pl.ds(0, 8), :], top_ref),
                (x_ref.at[:, pl.ds(ROWS - 8, 8), :], end_ref),
                (d_ref.at[pl.ds(0, 8), :], dtop_ref),
                (d_ref.at[pl.ds(ROWS - 8, 8), :], dend_ref),
                (stability_ref, calm_ref),
                (obs_hbm, obs_ref),
                (var_hbm, var_ref),
                (site_hbm, site_ref),
                (count_hbm, count_ref),
            )
        )
    ]
    for copy in copies:
        copy.start()
    sub_id = lax.broadcasted_iota(jnp.int32, (8, PATCH), 0)
    lane = lax.broadcasted_iota(jnp.int32, (8, PATCH), 1)
    for copy in copies:
        copy.wait()
    me = 2 * y + rep
    away = 2 * lax.rem(y + 2, SUBS) + rep
    side_at = pl.multiple_of(BLOCK * (2 * y + 1 - rep), 8)
    for l in range(LEVELS + 1):
        packed = jnp.zeros((8, PATCH), jnp.float32)
        for r in range(8):
            rows = slice(8 * r, 8 * r + 8)
            tile = edge_ref[l, rows, :] if l < LEVELS else dedge_ref[rows, :]
            turned = pltpu.roll(tile, lax.rem(16 * (r + 1 - rep), PATCH), 1)
            packed = jnp.where(lane // 16 == r, turned, packed)
        send_ref[pl.ds(side_at + 8 * l, 8), :] = packed
    for ok, step, rows_ref, d_rows, first in (
        (y > 0, -1, top_ref, dtop_ref, 0),
        (y < SUBS - 1, 1, end_ref, dend_ref, 8 - STEPS),
    ):
        at = pl.multiple_of(BLOCK * jnp.where(ok, me + 2 * step, away), 8)
        corner = pl.multiple_of(BLOCK * jnp.where(ok, 2 * (y + step) + 1 - rep, away), 8)
        for l in range(LEVELS):
            send_ref[pl.ds(corner + l, STEPS, stride=8), :] = edge_ref[
                l, (first // 4) * (ROWS - 8) + first : (first // 4) * (ROWS - 8) + first + STEPS, :
            ]
        send_ref[pl.ds(corner + 32, STEPS), :] = dedge_ref[
            (first // 4) * (ROWS - 8) + first : (first // 4) * (ROWS - 8) + first + STEPS, :
        ]
        for h in range(2):
            cols = slice(h * PATCH, (h + 1) * PATCH)
            for l in range(LEVELS):
                send_ref[pl.ds(at + 8 * h + l, STEPS, stride=16), :] = rows_ref[
                    l, first : first + STEPS, cols
                ]
            send_ref[pl.ds(at + 64 + STEPS * h, STEPS), :] = d_rows[first : first + STEPS, cols]
    own = pl.multiple_of(BLOCK * me, 8)
    picked = jnp.where(sub_id[:, :8] == lane[:, :8], calm_ref[...], 0.0)
    send_ref[pl.ds(own, 8), :] = jnp.broadcast_to(jnp.sum(picked, axis=1, keepdims=True), (LEVELS, PATCH))
    send_ref[pl.ds(own + 8, 2), :] = obs_ref[...]
    for p in range(2):
        live = lane[:1] < count_ref[:, p : p + 1]
        send_ref[pl.ds(own + 10 + p, 1), :] = jnp.where(live, 1.0 / var_ref[p : p + 1, :], 0.0)
    send_ref[pl.ds(own + 12, 2), :] = site_ref[...].astype(jnp.float32)


def forecast_kernel(x_ref, d_ref, got_ref, out_ref, slots_ref, a_ref, b_ref, w_ref):
    y, rep = lax.axis_index("sub"), lax.axis_index("rep")
    lane = lax.broadcasted_iota(jnp.int32, (8, PATCH), 1)
    low = jnp.where(rep == 0, 0, PATCH - STEPS)
    keep = (lane >= low) & (lane < low + STEPS)
    me = 2 * y + rep
    away = 2 * lax.rem(y + 2, SUBS) + rep
    side_at = pl.multiple_of(BLOCK * (2 * y + 1 - rep), 8)
    own = 24 * STEPS
    for l in range(LEVELS + 1):
        packed = got_ref[pl.ds(side_at + 8 * l, 8), :]
        for r in range(8):
            turned = pltpu.roll(packed, lax.rem(PATCH - 16 * (r + rep), PATCH), 1)
            side = jnp.where(keep, turned, 0.0)
            if l < LEVELS:
                a_ref[pl.ds(own + 24 * 8 * r + 16 + l, 8, stride=24), :] = side
            else:
                w_ref[168 + 8 * r : 176 + 8 * r, :] = side
    for l in range(LEVELS):
        for t in range(2):
            a_ref[pl.ds(own + 8 * t + l, ROWS, stride=24), :] = x_ref[
                ROWS * l : ROWS * (l + 1), t * PATCH : (t + 1) * PATCH
            ]
    for t in range(2):
        w_ref[80 * t + 8 : 80 * t + 8 + ROWS, :] = d_ref[:, t * PATCH : (t + 1) * PATCH]
    for ok, step, base, d_base in (
        (y > 0, -1, 0, STEPS),
        (y < SUBS - 1, 1, STEPS + ROWS, 8 + ROWS),
    ):
        at = pl.multiple_of(BLOCK * jnp.where(ok, me + 2 * step, away), 8)
        corner = pl.multiple_of(BLOCK * jnp.where(ok, 2 * (y + step) + 1 - rep, away), 8)
        there = jnp.broadcast_to(ok, (8, PATCH))
        both = keep & there
        for r in range(STEPS):
            to = 24 * (base + r)
            for t in range(2):
                a_ref[to + 8 * t : to + 8 * t + 8, :] = jnp.where(
                    there, got_ref[pl.ds(at + 16 * r + 8 * t, 8), :], 0.0
                )
            a_ref[to + 16 : to + 24, :] = jnp.where(both, got_ref[pl.ds(corner + 8 * r, 8), :], 0.0)
        rows = jnp.where(there, got_ref[pl.ds(at + 64, 8), :], 0.0)
        for t in range(2):
            w_ref[80 * t + d_base : 80 * t + d_base + STEPS, :] = rows[STEPS * t : STEPS * (t + 1)]
        rows = jnp.where(both, got_ref[pl.ds(corner + 32, 8), :], 0.0)
        w_ref[160 + d_base : 160 + d_base + STEPS, :] = rows[:STEPS]
    mine = pl.multiple_of(BLOCK * me, 8)
    wind = got_ref[pl.ds(mine, 8), :]
    slots_ref[...] = got_ref[pl.ds(mine + 8, 8), :]
    winds = [wind, wind, jnp.where(keep, wind, 0.0)]
    first_lane, last_lane = lane == 0, lane == PATCH - 1

    for step in range(STEPS):
        src, dst = (a_ref, b_ref) if step % 2 == 0 else (b_ref, a_ref)
        final = step == STEPS - 1
        skip = STEPS if final else step + 1

        def tiles(row):
            return [src[24 * row + 8 * t : 24 * row + 8 * t + 8, :] for t in range(3)]

        northern, centre = tiles(skip - 1), tiles(skip)
        for row in range(skip, TALL - skip):
            southern = tiles(row + 1)
            right = [pltpu.roll(v, 1, 1) for v in centre]
            left = [pltpu.roll(v, PATCH - 1, 1) for v in centre]
            for t in range(2 if final else 3):
                west = jnp.where(first_lane, right[(t + 2) % 3], right[t])
                east = jnp.where(last_lane, left[(t + 1) % 3], left[t])
                spread = northern[t] + southern[t] + (west + east) - 4.0 * centre[t]
                d_row = w_ref[80 * t + row + STEPS : 80 * t + row + STEPS + 1, :]
                new = centre[t] + d_row * spread - winds[t] * (centre[t] - west)
                if final:
                    at = 16 * (row - skip) + 8 * t
                    out_ref[at : at + 8, :] = new
                else:
                    at = 24 * row + 8 * t
                    dst[at : at + 8, :] = new
            northern, centre = centre, southern


def analysis_kernel(x_ref, slots_ref, out_ref, pert_ref):
    members = MEMBERS
    both = 2 * members
    lanes = lax.broadcasted_iota(jnp.int32, (8, PATCH), 1)
    site = slots_ref[4:6, :].astype(jnp.int32)
    level = site // PATCH
    column = site - level * PATCH
    means = [[None] * LEVELS for _ in range(2)]
    perts, weighteds, forcings = [], [], []
    for p in range(2):
        pick = jnp.broadcast_to(column[p : p + 1, :], (members, PATCH))
        got = jnp.zeros((members, PATCH), jnp.float32)
        for l in range(LEVELS):
            block = x_ref[pl.ds(8 * p + l, members, stride=16), :]
            mean = jnp.sum(block, axis=0, keepdims=True) * (1.0 / members)
            means[p][l] = mean
            pert_ref[p * members : (p + 1) * members, l * PATCH : (l + 1) * PATCH] = block - mean
            here = jnp.take_along_axis(block, pick, axis=1, mode="promise_in_bounds")
            got = jnp.where(level[p : p + 1, :] == l, here, got)
        mean = jnp.sum(got, axis=0, keepdims=True) * (1.0 / members)
        pert = got - mean
        weighted = pert * slots_ref[2 + p : 3 + p, :]
        perts.append(pert)
        weighteds.append(weighted)
        innovation = slots_ref[p : p + 1, :] - mean
        forcings.append(jnp.sum(weighted * innovation, axis=1, keepdims=True))
    nt = (((1,), (1,)), ((), ()))
    cross = lax.dot_general(
        jnp.concatenate(weighteds, 0), jnp.concatenate(perts, 0), nt,
        precision=HIGHEST, preferred_element_type=jnp.float32,
    )
    row_id = lax.broadcasted_iota(jnp.int32, (both, both), 0)
    col_id = lax.broadcasted_iota(jnp.int32, (both, both), 1)
    eye = (row_id == col_id).astype(jnp.float32)
    system = jnp.where((row_id < members) == (col_id < members), cross, 0.0) + (members - 1.0) * eye
    moved = []

    def spread_steps():
        def mm(a, b):
            return jnp.dot(a, b, precision=HIGHEST, preferred_element_type=jnp.float32)

        squares = jnp.sum(system * system, axis=1, keepdims=True)
        norms = [
            jnp.sqrt(jnp.sum(squares[p * members : (p + 1) * members], axis=0, keepdims=True))
            for p in range(2)
        ]
        norm = jnp.where(row_id[:, :1] < members, norms[0], norms[1])
        iterate = system / norm
        root = update = 1.5 * eye - 0.5 * iterate
        for sweep in range(1, NS_ITERS):
            iterate = mm(iterate, update)
            yield
            update = 1.5 * eye - 0.5 * mm(root, iterate)
            yield
            root = mm(update, root)
            yield
        spread = root * jnp.sqrt((members - 1.0) / norm)
        tn = (((0,), (0,)), ((), ()))
        for l in range(LEVELS):
            moved.append(
                lax.dot_general(
                    spread, pert_ref[:, l * PATCH : (l + 1) * PATCH], tn,
                    precision=HIGHEST, preferred_element_type=jnp.float32,
                )
            )
            yield

    m = system[:members, :] + system[members:, :]
    left = lanes < members
    m = [m[8 * q : 8 * q + 8, :] for q in range(8)]
    f = [
        jnp.where(left, forcings[0][8 * q : 8 * q + 8, :], forcings[1][8 * q : 8 * q + 8, :])
        for q in range(8)
    ]
    sub_id = lax.broadcasted_iota(jnp.int32, (8, PATCH), 0)
    even = sub_id % 2 == 0
    same = [None] * 8
    other = [None] * 8
    steps = spread_steps()
    for k in range(0, members, 2):
        next(steps, None)
        q, r = divmod(k, 8)
        c0, c1 = (
            [jnp.take_along_axis(v, jnp.where(left, j, members + j), axis=1, mode="promise_in_bounds") for v in m]
            for j in (k, k + 1)
        )
        a, b, d = c0[q][r : r + 1, :], c0[q][r + 1 : r + 2, :], c1[q][r + 1 : r + 2, :]
        inv = 1.0 / (a * d - b * b)
        a, b, d = a * inv, b * inv, d * inv
        pair = (sub_id // 2) * 2 == r
        keep_same, keep_other = jnp.where(even, d, a), jnp.broadcast_to(-b, (8, PATCH))
        same[q] = keep_same if r == 0 else jnp.where(pair, keep_same, same[q])
        other[q] = keep_other if r == 0 else jnp.where(pair, keep_other, other[q])
        r0, r1 = m[q][r : r + 1, :], m[q][r + 1 : r + 2, :]
        f0, f1 = f[q][r : r + 1, :], f[q][r + 1 : r + 2, :]
        c0[q], c1[q] = jnp.where(pair, 0.0, c0[q]), jnp.where(pair, 0.0, c1[q])
        r0, r1 = d * r0 - b * r1, a * r1 - b * r0
        f0, f1 = d * f0 - b * f1, a * f1 - b * f0
        m = [v - (u * r0 + w * r1) for v, u, w in zip(m, c0, c1)]
        f = [v - (u * f0 + w * f1) for v, u, w in zip(f, c0, c1)]
    for _ in steps:
        pass
    weight = []
    for q in range(8):
        partner = jnp.where(even, pltpu.roll(f[q], 7, 0), pltpu.roll(f[q], 1, 0))
        weight.append(same[q] * f[q] + other[q] * partner)
    weight = jnp.concatenate(weight, 0)
    turned = pltpu.roll(weight, members, 1)
    left_all = col_id[:members] < members
    for p in range(2):
        wide = jnp.where(left_all, weight, turned) if p == 0 else jnp.where(left_all, turned, weight)
        for l in range(LEVELS):
            rows = slice(p * members, (p + 1) * members)
            shift = jnp.sum(wide * pert_ref[rows, l * PATCH : (l + 1) * PATCH], axis=0, keepdims=True)
            out_ref[pl.ds(8 * p + l, members, stride=16), :] = moved[l][rows] + (means[p][l] + shift)


def unpack_kernel(x_ref, out_ref):
    for l in range(LEVELS):
        for h in range(2):
            out_ref[ROWS * l : ROWS * (l + 1), h * PATCH : (h + 1) * PATCH] = x_ref[
                pl.ds(8 * h + l, ROWS, stride=16), :
            ]


VMEM = pl.BlockSpec(memory_space=pltpu.VMEM)
SMEM = pl.BlockSpec(memory_space=pltpu.SMEM)
HBM = pl.BlockSpec(memory_space=pltpu.HBM)


def f32(*dims):
    return jax.ShapeDtypeStruct(dims, jnp.float32)


def call(kernel, outs, specs, scratch=(), flops=1_000_000, name=None, limit=VMEM_LIMIT):
    return pl.pallas_call(
        kernel,
        out_shape=outs if len(outs) > 1 else outs[0],
        in_specs=specs,
        out_specs=[VMEM] * len(outs) if len(outs) > 1 else VMEM,
        scratch_shapes=scratch,
        compiler_params=pltpu.CompilerParams(vmem_limit_bytes=limit),
        cost_estimate=pl.CostEstimate(flops=flops, bytes_accessed=1_000_000, transcendentals=0),
        name=name,
    )


def on_device(start, diffusivity, stability, observed, variance, site, live):
    def vmem(*dims, dtype=jnp.float32):
        return pltpu.VMEM(dims, dtype)

    send = call(
        pack_kernel,
        [f32(2 * SUBS * BLOCK, PATCH)],
        [HBM] * 7,
        scratch=[
            vmem(LEVELS, 8, COLS),
            vmem(LEVELS, 8, COLS),
            vmem(8, COLS),
            vmem(8, COLS),
            vmem(LEVELS, ROWS, PATCH),
            vmem(ROWS, PATCH),
            vmem(1, LEVELS),
            vmem(2, PATCH),
            vmem(2, PATCH),
            vmem(2, PATCH, dtype=jnp.int32),
            vmem(1, 2, dtype=jnp.int32),
            pltpu.SemaphoreType.DMA((11,)),
        ],
        name="pack",
        limit=PACK_LIMIT,
    )(
        start.reshape(LEVELS, ROWS, COLS),
        diffusivity,
        stability,
        observed.reshape(2, PATCH),
        variance.reshape(2, PATCH),
        site.reshape(2, PATCH),
        live,
    )
    got = lax.all_to_all(send.reshape(2 * SUBS, BLOCK, PATCH), ("sub", "rep"), 0, 0, tiled=True)
    forecast, slots = call(
        forecast_kernel,
        [f32(ROWS * 16, PATCH), f32(8, PATCH)],
        [VMEM] * 3,
        scratch=[vmem(24 * TALL, PATCH), vmem(24 * TALL, PATCH), vmem(3 * (ROWS + 16), PATCH)],
        name="forecast",
    )(start.reshape(LEVELS * ROWS, COLS), diffusivity, got.reshape(2 * SUBS * BLOCK, PATCH))
    gathered = lax.all_to_all(forecast.reshape(ROWS, 16, PATCH), GRP, 0, 0, tiled=True)
    analysed = call(
        analysis_kernel,
        [f32(MEMBERS * 16, PATCH)],
        [VMEM] * 2,
        scratch=[pltpu.VMEM((2 * MEMBERS, LEVELS * PATCH), jnp.float32)],
        name="analysis",
    )(gathered.reshape(MEMBERS * 16, PATCH), slots)
    returned = lax.all_to_all(analysed.reshape(MEMBERS, 16, PATCH), GRP, 0, 0, tiled=True)
    out = call(unpack_kernel, [f32(LEVELS * ROWS, COLS)], [VMEM], name="unpack")(
        returned.reshape(ROWS * 16, PATCH)
    )
    return out.reshape(1, LEVELS, ROWS, COLS)


def solution(mesh):
    split = Mesh(
        mesh.devices.reshape(16, 4, mesh.shape["sub"], mesh.shape["rep"]),
        ("grp_0", "grp_1", "sub", "rep"),
    )
    return jax.shard_map(
        on_device,
        mesh=split,
        in_specs=(
            P(GRP, None, "sub", "rep"),
            P("sub", "rep"),
            P(GRP, None),
            P(SUB_GRP, "rep", None),
            P(SUB_GRP, "rep", None),
            P(SUB_GRP, "rep", None),
            P(SUB_GRP, "rep"),
        ),
        out_specs=P(GRP, None, "sub", "rep"),
        check_vma=False,
    )
```

```python
import jax
import jax.numpy as jnp
from jax import lax
from jax.experimental import pallas as pl
from jax.experimental.pallas import tpu as pltpu
from jax.sharding import Mesh
from jax.sharding import PartitionSpec as P

LEVELS = 8
PATCH = 128
STEPS = 4
NS_ITERS = 4
MEMBERS = 64
ROWS = 64
COLS = 256
TALL = ROWS + 2 * STEPS
GRP = ("grp_0", "grp_1")
SUB_GRP = ("sub", "grp_0", "grp_1")
HIGHEST = lax.Precision.HIGHEST
VMEM_LIMIT = 24 * 1024 * 1024
SUBS = 4
BLOCK = 72


def pack_kernel(
    x_ref, d_ref, stability_ref, obs_hbm, var_hbm, site_hbm, count_hbm, send_ref,
    top_ref, end_ref, dtop_ref, dend_ref, edge_ref, dedge_ref, calm_ref, obs_ref, var_ref, site_ref, count_ref, sems,
):
    y, rep = lax.axis_index("sub"), lax.axis_index("rep")
    half = pl.ds(pl.multiple_of((1 - rep) * PATCH, PATCH), PATCH)
    copies = [
        pltpu.make_async_copy(src, dst, sems.at[i])
        for i, (src, dst) in enumerate(
            (
                (x_ref.at[:, :, half], edge_ref),
                (d_ref.at[:, half], dedge_ref),
                (x_ref.at[:, pl.ds(0, 8), :], top_ref),
                (x_ref.at[:, pl.ds(ROWS - 8, 8), :], end_ref),
                (d_ref.at[pl.ds(0, 8), :], dtop_ref),
                (d_ref.at[pl.ds(ROWS - 8, 8), :], dend_ref),
                (stability_ref, calm_ref),
                (obs_hbm, obs_ref),
                (var_hbm, var_ref),
                (site_hbm, site_ref),
                (count_hbm, count_ref),
            )
        )
    ]
    for copy in copies:
        copy.start()
    sub_id = lax.broadcasted_iota(jnp.int32, (8, PATCH), 0)
    lane = lax.broadcasted_iota(jnp.int32, (8, PATCH), 1)
    for copy in copies:
        copy.wait()
    me = 2 * y + rep
    away = 2 * lax.rem(y + 2, SUBS) + rep
    side_at = pl.multiple_of(BLOCK * (2 * y + 1 - rep), 8)
    for l in range(LEVELS + 1):
        packed = jnp.zeros((8, PATCH), jnp.float32)
        for r in range(8):
            rows = slice(8 * r, 8 * r + 8)
            tile = edge_ref[l, rows, :] if l < LEVELS else dedge_ref[rows, :]
            turned = pltpu.roll(tile, lax.rem(16 * (r + 1 - rep), PATCH), 1)
            packed = jnp.where(lane // 16 == r, turned, packed)
        send_ref[pl.ds(side_at + 8 * l, 8), :] = packed
    for ok, step, rows_ref, d_rows, first in (
        (y > 0, -1, top_ref, dtop_ref, 0),
        (y < SUBS - 1, 1, end_ref, dend_ref, 8 - STEPS),
    ):
        at = pl.multiple_of(BLOCK * jnp.where(ok, me + 2 * step, away), 8)
        corner = pl.multiple_of(BLOCK * jnp.where(ok, 2 * (y + step) + 1 - rep, away), 8)
        for l in range(LEVELS):
            send_ref[pl.ds(corner + l, STEPS, stride=8), :] = edge_ref[
                l, (first // 4) * (ROWS - 8) + first : (first // 4) * (ROWS - 8) + first + STEPS, :
            ]
        send_ref[pl.ds(corner + 32, STEPS), :] = dedge_ref[
            (first // 4) * (ROWS - 8) + first : (first // 4) * (ROWS - 8) + first + STEPS, :
        ]
        for h in range(2):
            cols = slice(h * PATCH, (h + 1) * PATCH)
            for l in range(LEVELS):
                send_ref[pl.ds(at + 8 * h + l, STEPS, stride=16), :] = rows_ref[
                    l, first : first + STEPS, cols
                ]
            send_ref[pl.ds(at + 64 + STEPS * h, STEPS), :] = d_rows[first : first + STEPS, cols]
    own = pl.multiple_of(BLOCK * me, 8)
    picked = jnp.where(sub_id[:, :8] == lane[:, :8], calm_ref[...], 0.0)
    send_ref[pl.ds(own, 8), :] = jnp.broadcast_to(jnp.sum(picked, axis=1, keepdims=True), (LEVELS, PATCH))
    send_ref[pl.ds(own + 8, 2), :] = obs_ref[...]
    for p in range(2):
        live = lane[:1] < count_ref[:, p : p + 1]
        send_ref[pl.ds(own + 10 + p, 1), :] = jnp.where(live, 1.0 / var_ref[p : p + 1, :], 0.0)
    send_ref[pl.ds(own + 12, 2), :] = site_ref[...].astype(jnp.float32)


def forecast_kernel(x_ref, d_ref, got_ref, out_ref, slots_ref, a_ref, b_ref, w_ref):
    y, rep = lax.axis_index("sub"), lax.axis_index("rep")
    lane = lax.broadcasted_iota(jnp.int32, (8, PATCH), 1)
    low = jnp.where(rep == 0, 0, PATCH - STEPS)
    keep = (lane >= low) & (lane < low + STEPS)
    me = 2 * y + rep
    away = 2 * lax.rem(y + 2, SUBS) + rep
    side_at = pl.multiple_of(BLOCK * (2 * y + 1 - rep), 8)
    own = 24 * STEPS
    for l in range(LEVELS + 1):
        packed = got_ref[pl.ds(side_at + 8 * l, 8), :]
        for r in range(8):
            turned = pltpu.roll(packed, lax.rem(PATCH - 16 * (r + rep), PATCH), 1)
            side = jnp.where(keep, turned, 0.0)
            if l < LEVELS:
                a_ref[pl.ds(own + 24 * 8 * r + 16 + l, 8, stride=24), :] = side
            else:
                w_ref[168 + 8 * r : 176 + 8 * r, :] = side
    for l in range(LEVELS):
        for t in range(2):
            a_ref[pl.ds(own + 8 * t + l, ROWS, stride=24), :] = x_ref[
                ROWS * l : ROWS * (l + 1), t * PATCH : (t + 1) * PATCH
            ]
    for t in range(2):
        w_ref[80 * t + 8 : 80 * t + 8 + ROWS, :] = d_ref[:, t * PATCH : (t + 1) * PATCH]
    for ok, step, base, d_base in (
        (y > 0, -1, 0, STEPS),
        (y < SUBS - 1, 1, STEPS + ROWS, 8 + ROWS),
    ):
        at = pl.multiple_of(BLOCK * jnp.where(ok, me + 2 * step, away), 8)
        corner = pl.multiple_of(BLOCK * jnp.where(ok, 2 * (y + step) + 1 - rep, away), 8)
        there = jnp.broadcast_to(ok, (8, PATCH))
        both = keep & there
        for r in range(STEPS):
            to = 24 * (base + r)
            for t in range(2):
                a_ref[to + 8 * t : to + 8 * t + 8, :] = jnp.where(
                    there, got_ref[pl.ds(at + 16 * r + 8 * t, 8), :], 0.0
                )
            a_ref[to + 16 : to + 24, :] = jnp.where(both, got_ref[pl.ds(corner + 8 * r, 8), :], 0.0)
        rows = jnp.where(there, got_ref[pl.ds(at + 64, 8), :], 0.0)
        for t in range(2):
            w_ref[80 * t + d_base : 80 * t + d_base + STEPS, :] = rows[STEPS * t : STEPS * (t + 1)]
        rows = jnp.where(both, got_ref[pl.ds(corner + 32, 8), :], 0.0)
        w_ref[160 + d_base : 160 + d_base + STEPS, :] = rows[:STEPS]
    mine = pl.multiple_of(BLOCK * me, 8)
    wind = got_ref[pl.ds(mine, 8), :]
    slots_ref[...] = got_ref[pl.ds(mine + 8, 8), :]
    winds = [wind, wind, jnp.where(keep, wind, 0.0)]
    first_lane, last_lane = lane == 0, lane == PATCH - 1

    for step in range(STEPS):
        src, dst = (a_ref, b_ref) if step % 2 == 0 else (b_ref, a_ref)
        final = step == STEPS - 1
        skip = STEPS if final else step + 1

        def tiles(row):
            return [src[24 * row + 8 * t : 24 * row + 8 * t + 8, :] for t in range(3)]

        northern, centre = tiles(skip - 1), tiles(skip)
        for row in range(skip, TALL - skip):
            southern = tiles(row + 1)
            right = [pltpu.roll(v, 1, 1) for v in centre]
            left = [pltpu.roll(v, PATCH - 1, 1) for v in centre]
            for t in range(2 if final else 3):
                west = jnp.where(first_lane, right[(t + 2) % 3], right[t])
                east = jnp.where(last_lane, left[(t + 1) % 3], left[t])
                spread = northern[t] + southern[t] + (west + east) - 4.0 * centre[t]
                d_row = w_ref[80 * t + row + STEPS : 80 * t + row + STEPS + 1, :]
                new = centre[t] + d_row * spread - winds[t] * (centre[t] - west)
                if final:
                    at = 16 * (row - skip) + 8 * t
                    out_ref[at : at + 8, :] = new
                else:
                    at = 24 * row + 8 * t
                    dst[at : at + 8, :] = new
            northern, centre = centre, southern


def analysis_kernel(x_ref, slots_ref, out_ref, pert_ref):
    members = MEMBERS
    both = 2 * members
    tile = (8, PATCH)
    lanes = lax.broadcasted_iota(jnp.int32, tile, 1)
    sub_id = lax.broadcasted_iota(jnp.int32, tile, 0)
    left = lanes < members
    site = slots_ref[4:6, :].astype(jnp.int32)
    level = site // PATCH
    column = site - level * PATCH
    perts, weighteds, forcings = [], [], []
    for p in range(2):
        pick = jnp.broadcast_to(column[p : p + 1, :], (members, PATCH))
        got = None
        for l in range(LEVELS):
            block = x_ref[pl.ds(8 * p + l, members, stride=16), :]
            here = jnp.take_along_axis(block, pick, axis=1, mode="promise_in_bounds")
            got = here if got is None else jnp.where(level[p : p + 1, :] == l, here, got)
        mean = jnp.sum(got, axis=0, keepdims=True) * (1.0 / members)
        pert = got - mean
        weighted = pert * slots_ref[2 + p : 3 + p, :]
        perts.append(pert)
        weighteds.append(weighted)
        innovation = slots_ref[p : p + 1, :] - mean
        forcings.append(jnp.sum(weighted * innovation, axis=1, keepdims=True))
    nt = (((1,), (1,)), ((), ()))
    zero = jnp.zeros((members, PATCH), jnp.float32)
    pair = jnp.concatenate(
        [jnp.concatenate([perts[0], zero], 1), jnp.concatenate([zero, perts[1]], 1)], 0
    )
    cross = lax.dot_general(
        jnp.concatenate(weighteds, 1), pair, nt,
        precision=HIGHEST, preferred_element_type=jnp.float32,
    )
    row_id = lax.broadcasted_iota(jnp.int32, (members, PATCH), 0)
    col_id = lax.broadcasted_iota(jnp.int32, (members, PATCH), 1)
    left_all = col_id < members
    on_diagonal = row_id == col_id - jnp.where(left_all, 0, members)
    m = cross + jnp.where(on_diagonal, members - 1.0, 0.0)
    system = jnp.concatenate([jnp.where(left_all, m, 0.0), jnp.where(left_all, 0.0, m)], 0)
    means = [[None] * LEVELS for _ in range(2)]
    moved = []

    def spread_steps():
        def mm(a, b):
            return jnp.dot(a, b, precision=HIGHEST, preferred_element_type=jnp.float32)

        def centre(l):
            for p in range(2):
                block = x_ref[pl.ds(8 * p + l, members, stride=16), :]
                mean = jnp.sum(block, axis=0, keepdims=True) * (1.0 / members)
                means[p][l] = mean
                pert_ref[p * members : (p + 1) * members, l * PATCH : (l + 1) * PATCH] = block - mean

        squares = jnp.sum(system * system, axis=1, keepdims=True)
        norms = [
            jnp.sqrt(jnp.sum(squares[p * members : (p + 1) * members], axis=0, keepdims=True))
            for p in range(2)
        ]
        first_half = lax.broadcasted_iota(jnp.int32, (both, 1), 0) < members
        norm = jnp.where(first_half, norms[0], norms[1])
        eye = (
            lax.broadcasted_iota(jnp.int32, (both, both), 0)
            == lax.broadcasted_iota(jnp.int32, (both, both), 1)
        ).astype(jnp.float32)
        iterate = system / norm
        root = update = 1.5 * eye - 0.5 * iterate
        for sweep in range(1, NS_ITERS):
            iterate = mm(iterate, update)
            centre(3 * sweep - 3)
            yield
            update = 1.5 * eye - 0.5 * mm(root, iterate)
            centre(3 * sweep - 2)
            yield
            root = mm(update, root)
            if 3 * sweep - 1 < LEVELS:
                centre(3 * sweep - 1)
            yield
        spread = root * jnp.sqrt((members - 1.0) / norm)
        tn = (((0,), (0,)), ((), ()))
        for l in range(LEVELS):
            moved.append(
                lax.dot_general(
                    spread, pert_ref[:, l * PATCH : (l + 1) * PATCH], tn,
                    precision=HIGHEST, preferred_element_type=jnp.float32,
                )
            )
            yield

    m = [m[8 * q : 8 * q + 8, :] for q in range(8)]
    f = [
        jnp.where(left, forcings[0][8 * q : 8 * q + 8, :], forcings[1][8 * q : 8 * q + 8, :])
        for q in range(8)
    ]
    inverse = [[None] * 4 for _ in range(8)]
    steps = spread_steps()

    def spread_row(v, row):
        return jnp.broadcast_to(v[row : row + 1, :], tile)

    for k in range(0, members, 4):
        next(steps, None)
        q, r = divmod(k, 8)
        c = [
            [jnp.take_along_axis(v, jnp.where(left, j, members + j), axis=1, mode="promise_in_bounds") for v in m]
            for j in range(k, k + 4)
        ]
        b = [[spread_row(c[j][q], r + i) for j in range(4)] for i in range(4)]
        det = 1.0 / (b[0][0] * b[1][1] - b[0][1] * b[0][1])
        a00, a01, a11 = b[1][1] * det, -b[0][1] * det, b[0][0] * det
        e00, e01 = a00 * b[0][2] + a01 * b[1][2], a00 * b[0][3] + a01 * b[1][3]
        e10, e11 = a01 * b[0][2] + a11 * b[1][2], a01 * b[0][3] + a11 * b[1][3]
        s00 = b[2][2] - (b[0][2] * e00 + b[1][2] * e10)
        s01 = b[2][3] - (b[0][2] * e01 + b[1][2] * e11)
        s11 = b[3][3] - (b[0][3] * e01 + b[1][3] * e11)
        det = 1.0 / (s00 * s11 - s01 * s01)
        t00, t01, t11 = s11 * det, -s01 * det, s00 * det
        g00, g01 = e00 * t00 + e01 * t01, e00 * t01 + e01 * t11
        g10, g11 = e10 * t00 + e11 * t01, e10 * t01 + e11 * t11
        x01 = a01 + (g00 * e10 + g01 * e11)
        x = [
            [a00 + (g00 * e00 + g01 * e01), x01, -g00, -g01],
            [x01, a11 + (g10 * e10 + g11 * e11), -g10, -g11],
            [-g00, -g10, t00, t01],
            [-g01, -g11, t01, t11],
        ]
        rows = [spread_row(m[q], r + i) for i in range(4)]
        loads = [spread_row(f[q], r + i) for i in range(4)]
        for j in range(4):
            for i in range(4):
                old = inverse[q][j]
                inverse[q][j] = x[i][j] if old is None else jnp.where(sub_id == r + i, x[i][j], old)
        rows = [(x[i][0] * rows[0] + x[i][1] * rows[1]) + (x[i][2] * rows[2] + x[i][3] * rows[3]) for i in range(4)]
        loads = [(x[i][0] * loads[0] + x[i][1] * loads[1]) + (x[i][2] * loads[2] + x[i][3] * loads[3]) for i in range(4)]
        pivot = (sub_id >= r) & (sub_id < r + 4)
        for i in range(4):
            c[i][q] = jnp.where(pivot, 0.0, c[i][q])
        if k < members - 4:
            m = [
                m[n] - ((c[0][n] * rows[0] + c[1][n] * rows[1]) + (c[2][n] * rows[2] + c[3][n] * rows[3]))
                for n in range(8)
            ]
        f = [
            f[n] - ((c[0][n] * loads[0] + c[1][n] * loads[1]) + (c[2][n] * loads[2] + c[3][n] * loads[3]))
            for n in range(8)
        ]
    for _ in steps:
        pass
    weight = []
    for q in range(8):
        terms = [
            inverse[q][j] * jnp.where(sub_id < 4, f[q][j : j + 1, :], f[q][4 + j : 5 + j, :])
            for j in range(4)
        ]
        weight.append((terms[0] + terms[1]) + (terms[2] + terms[3]))
    weight = jnp.concatenate(weight, 0)
    turned = pltpu.roll(weight, members, 1)
    for p in range(2):
        wide = jnp.where(left_all, weight, turned) if p == 0 else jnp.where(left_all, turned, weight)
        for l in range(LEVELS):
            rows = slice(p * members, (p + 1) * members)
            shift = jnp.sum(wide * pert_ref[rows, l * PATCH : (l + 1) * PATCH], axis=0, keepdims=True)
            out_ref[pl.ds(8 * p + l, members, stride=16), :] = moved[l][rows] + (means[p][l] + shift)


def unpack_kernel(x_ref, out_hbm, out_ref, sems):
    copies = []
    for l in range(LEVELS):
        rows = slice(ROWS * l, ROWS * (l + 1))
        for h in range(2):
            out_ref[rows, h * PATCH : (h + 1) * PATCH] = x_ref[pl.ds(8 * h + l, ROWS, stride=16), :]
        if l % 2:
            some = pl.ds(ROWS * (l - 1), 2 * ROWS)
            copies.append(pltpu.make_async_copy(out_ref.at[some], out_hbm.at[some], sems.at[l // 2]))
            copies[-1].start()
    for copy in copies:
        copy.wait()


VMEM = pl.BlockSpec(memory_space=pltpu.VMEM)
SMEM = pl.BlockSpec(memory_space=pltpu.SMEM)
HBM = pl.BlockSpec(memory_space=pltpu.HBM)


def f32(*dims):
    return jax.ShapeDtypeStruct(dims, jnp.float32)


def call(kernel, outs, specs, scratch=(), flops=1_000_000, name=None, to=VMEM):
    return pl.pallas_call(
        kernel,
        out_shape=outs if len(outs) > 1 else outs[0],
        in_specs=specs,
        out_specs=[to] * len(outs) if len(outs) > 1 else to,
        scratch_shapes=scratch,
        compiler_params=pltpu.CompilerParams(vmem_limit_bytes=VMEM_LIMIT),
        cost_estimate=pl.CostEstimate(flops=flops, bytes_accessed=1_000_000, transcendentals=0),
        name=name,
    )


def on_device(start, diffusivity, stability, observed, variance, site, live):
    def vmem(*dims, dtype=jnp.float32):
        return pltpu.VMEM(dims, dtype)

    send = call(
        pack_kernel,
        [f32(2 * SUBS * BLOCK, PATCH)],
        [HBM] * 7,
        scratch=[
            vmem(LEVELS, 8, COLS),
            vmem(LEVELS, 8, COLS),
            vmem(8, COLS),
            vmem(8, COLS),
            vmem(LEVELS, ROWS, PATCH),
            vmem(ROWS, PATCH),
            vmem(1, LEVELS),
            vmem(2, PATCH),
            vmem(2, PATCH),
            vmem(2, PATCH, dtype=jnp.int32),
            vmem(1, 2, dtype=jnp.int32),
            pltpu.SemaphoreType.DMA((11,)),
        ],
        name="pack",
    )(
        *(
            pltpu.with_memory_space_constraint(v, pltpu.HBM)
            for v in (
                start.reshape(LEVELS, ROWS, COLS),
                diffusivity,
                stability,
                observed.reshape(2, PATCH),
                variance.reshape(2, PATCH),
                site.reshape(2, PATCH),
                live,
            )
        )
    )
    got = lax.all_to_all(send.reshape(2 * SUBS, BLOCK, PATCH), ("sub", "rep"), 0, 0, tiled=True)
    forecast, slots = call(
        forecast_kernel,
        [f32(ROWS * 16, PATCH), f32(8, PATCH)],
        [VMEM] * 3,
        scratch=[vmem(24 * TALL, PATCH), vmem(24 * TALL, PATCH), vmem(3 * (ROWS + 16), PATCH)],
        name="forecast",
    )(start.reshape(LEVELS * ROWS, COLS), diffusivity, got.reshape(2 * SUBS * BLOCK, PATCH))
    gathered = lax.all_to_all(forecast.reshape(ROWS, 16, PATCH), GRP, 0, 0, tiled=True)
    analysed = call(
        analysis_kernel,
        [f32(MEMBERS * 16, PATCH)],
        [VMEM] * 2,
        scratch=[pltpu.VMEM((2 * MEMBERS, LEVELS * PATCH), jnp.float32)],
        name="analysis",
    )(gathered.reshape(MEMBERS * 16, PATCH), slots)
    returned = lax.all_to_all(analysed.reshape(MEMBERS, 16, PATCH), GRP, 0, 0, tiled=True)
    out = call(
        unpack_kernel,
        [f32(LEVELS * ROWS, COLS)],
        [VMEM],
        scratch=[vmem(LEVELS * ROWS, COLS), pltpu.SemaphoreType.DMA((LEVELS // 2,))],
        name="unpack",
        to=HBM,
    )(
        returned.reshape(ROWS * 16, PATCH)
    )
    return out.reshape(1, LEVELS, ROWS, COLS)


def solution(mesh):
    split = Mesh(
        mesh.devices.reshape(16, 4, mesh.shape["sub"], mesh.shape["rep"]),
        ("grp_0", "grp_1", "sub", "rep"),
    )
    return jax.shard_map(
        on_device,
        mesh=split,
        in_specs=(
            P(GRP, None, "sub", "rep"),
            P("sub", "rep"),
            P(GRP, None),
            P(SUB_GRP, "rep", None),
            P(SUB_GRP, "rep", None),
            P(SUB_GRP, "rep", None),
            P(SUB_GRP, "rep"),
        ),
        out_specs=P(GRP, None, "sub", "rep"),
        check_vma=False,
    )
```

```python
import jax
import jax.numpy as jnp
from jax import lax
from jax.experimental import pallas as pl
from jax.experimental.pallas import tpu as pltpu
from jax.sharding import Mesh
from jax.sharding import PartitionSpec as P

LEVELS = 8
PATCH = 128
STEPS = 4
NS_ITERS = 4
MEMBERS = 64
ROWS = 64
COLS = 256
TALL = ROWS + 2 * STEPS
GRP = ("grp_0", "grp_1")
SUB_GRP = ("sub", "grp_0", "grp_1")
HIGHEST = lax.Precision.HIGHEST
VMEM_LIMIT = 24 * 1024 * 1024
SUBS = 4
BLOCK = 72
TURN = 44


def pack_kernel(
    x_ref, d_ref, stability_ref, obs_hbm, var_hbm, site_hbm, count_hbm, send_ref,
    top_ref, end_ref, dtop_ref, dend_ref, edge_ref, dedge_ref, calm_ref, obs_ref, var_ref, site_ref, count_ref, sems,
):
    y, rep = lax.axis_index("sub"), lax.axis_index("rep")
    half = pl.ds(pl.multiple_of((1 - rep) * PATCH, PATCH), PATCH)
    copies = [
        pltpu.make_async_copy(src, dst, sems.at[i])
        for i, (src, dst) in enumerate(
            (
                (x_ref.at[:, :, half], edge_ref),
                (d_ref.at[:, half], dedge_ref),
                (x_ref.at[:, pl.ds(0, 8), :], top_ref),
                (x_ref.at[:, pl.ds(ROWS - 8, 8), :], end_ref),
                (d_ref.at[pl.ds(0, 8), :], dtop_ref),
                (d_ref.at[pl.ds(ROWS - 8, 8), :], dend_ref),
                (stability_ref, calm_ref),
                (obs_hbm, obs_ref),
                (var_hbm, var_ref),
                (site_hbm, site_ref),
                (count_hbm, count_ref),
            )
        )
    ]
    for copy in copies:
        copy.start()
    sub_id = lax.broadcasted_iota(jnp.int32, (8, PATCH), 0)
    lane = lax.broadcasted_iota(jnp.int32, (8, PATCH), 1)
    for copy in copies:
        copy.wait()
    me = 2 * y + rep
    away = 2 * lax.rem(y + 2, SUBS) + rep
    side_at = pl.multiple_of(BLOCK * (2 * y + 1 - rep), 8)
    for l in range(LEVELS + 1):
        packed = jnp.zeros((8, PATCH), jnp.float32)
        for r in range(8):
            rows = slice(8 * r, 8 * r + 8)
            tile = edge_ref[l, rows, :] if l < LEVELS else dedge_ref[rows, :]
            turned = pltpu.roll(tile, lax.rem(16 * (r + 1 - rep), PATCH), 1)
            packed = jnp.where(lane // 16 == r, turned, packed)
        send_ref[pl.ds(side_at + 8 * l, 8), :] = packed
    for ok, step, rows_ref, d_rows, first in (
        (y > 0, -1, top_ref, dtop_ref, 0),
        (y < SUBS - 1, 1, end_ref, dend_ref, 8 - STEPS),
    ):
        at = pl.multiple_of(BLOCK * jnp.where(ok, me + 2 * step, away), 8)
        corner = pl.multiple_of(BLOCK * jnp.where(ok, 2 * (y + step) + 1 - rep, away), 8)
        for l in range(LEVELS):
            send_ref[pl.ds(corner + l, STEPS, stride=8), :] = edge_ref[
                l, (first // 4) * (ROWS - 8) + first : (first // 4) * (ROWS - 8) + first + STEPS, :
            ]
        send_ref[pl.ds(corner + 32, STEPS), :] = dedge_ref[
            (first // 4) * (ROWS - 8) + first : (first // 4) * (ROWS - 8) + first + STEPS, :
        ]
        for h in range(2):
            cols = slice(h * PATCH, (h + 1) * PATCH)
            for l in range(LEVELS):
                send_ref[pl.ds(at + 8 * h + l, STEPS, stride=16), :] = rows_ref[
                    l, first : first + STEPS, cols
                ]
            send_ref[pl.ds(at + 64 + STEPS * h, STEPS), :] = d_rows[first : first + STEPS, cols]
    own = pl.multiple_of(BLOCK * me, 8)
    picked = jnp.where(sub_id[:, :8] == lane[:, :8], calm_ref[...], 0.0)
    send_ref[pl.ds(own, 8), :] = jnp.broadcast_to(jnp.sum(picked, axis=1, keepdims=True), (LEVELS, PATCH))
    send_ref[pl.ds(own + 8, 2), :] = obs_ref[...]
    for p in range(2):
        live = lane[:1] < count_ref[:, p : p + 1]
        send_ref[pl.ds(own + 10 + p, 1), :] = jnp.where(live, 1.0 / var_ref[p : p + 1, :], 0.0)
    send_ref[pl.ds(own + 12, 2), :] = site_ref[...].astype(jnp.float32)


def forecast_kernel(x_ref, d_ref, got_ref, out_ref, slots_ref, a_ref, b_ref, w_ref):
    y, rep = lax.axis_index("sub"), lax.axis_index("rep")
    lane = lax.broadcasted_iota(jnp.int32, (8, PATCH), 1)
    low = jnp.where(rep == 0, 0, PATCH - STEPS)
    keep = (lane >= low) & (lane < low + STEPS)
    me = 2 * y + rep
    away = 2 * lax.rem(y + 2, SUBS) + rep
    side_at = pl.multiple_of(BLOCK * (2 * y + 1 - rep), 8)
    own = 24 * STEPS
    for l in range(LEVELS + 1):
        packed = got_ref[pl.ds(side_at + 8 * l, 8), :]
        for r in range(8):
            turned = pltpu.roll(packed, lax.rem(PATCH - 16 * (r + rep), PATCH), 1)
            side = jnp.where(keep, turned, 0.0)
            if l < LEVELS:
                a_ref[pl.ds(own + 24 * 8 * r + 16 + l, 8, stride=24), :] = side
            else:
                w_ref[168 + 8 * r : 176 + 8 * r, :] = side
    for l in range(LEVELS):
        for t in range(2):
            a_ref[pl.ds(own + 8 * t + l, ROWS, stride=24), :] = x_ref[
                ROWS * l : ROWS * (l + 1), t * PATCH : (t + 1) * PATCH
            ]
    for t in range(2):
        w_ref[80 * t + 8 : 80 * t + 8 + ROWS, :] = d_ref[:, t * PATCH : (t + 1) * PATCH]
    for ok, step, base, d_base in (
        (y > 0, -1, 0, STEPS),
        (y < SUBS - 1, 1, STEPS + ROWS, 8 + ROWS),
    ):
        at = pl.multiple_of(BLOCK * jnp.where(ok, me + 2 * step, away), 8)
        corner = pl.multiple_of(BLOCK * jnp.where(ok, 2 * (y + step) + 1 - rep, away), 8)
        there = jnp.broadcast_to(ok, (8, PATCH))
        both = keep & there
        for r in range(STEPS):
            to = 24 * (base + r)
            for t in range(2):
                a_ref[to + 8 * t : to + 8 * t + 8, :] = jnp.where(
                    there, got_ref[pl.ds(at + 16 * r + 8 * t, 8), :], 0.0
                )
            a_ref[to + 16 : to + 24, :] = jnp.where(both, got_ref[pl.ds(corner + 8 * r, 8), :], 0.0)
        rows = jnp.where(there, got_ref[pl.ds(at + 64, 8), :], 0.0)
        for t in range(2):
            w_ref[80 * t + d_base : 80 * t + d_base + STEPS, :] = rows[STEPS * t : STEPS * (t + 1)]
        rows = jnp.where(both, got_ref[pl.ds(corner + 32, 8), :], 0.0)
        w_ref[160 + d_base : 160 + d_base + STEPS, :] = rows[:STEPS]
    mine = pl.multiple_of(BLOCK * me, 8)
    wind = got_ref[pl.ds(mine, 8), :]
    slots_ref[...] = got_ref[pl.ds(mine + 8, 8), :]
    winds = [wind, wind, jnp.where(keep, wind, 0.0)]
    first_lane, last_lane = lane == 0, lane == PATCH - 1

    for step in range(STEPS):
        src, dst = (a_ref, b_ref) if step % 2 == 0 else (b_ref, a_ref)
        final = step == STEPS - 1
        skip = STEPS if final else step + 1

        def tiles(row):
            return [src[24 * row + 8 * t : 24 * row + 8 * t + 8, :] for t in range(3)]

        northern, centre = tiles(skip - 1), tiles(skip)
        for row in range(skip, TALL - skip):
            southern = tiles(row + 1)
            right = [pltpu.roll(v, 1, 1) for v in centre]
            left = [pltpu.roll(v, PATCH - 1, 1) for v in centre]
            for t in range(2 if final else 3):
                west = jnp.where(first_lane, right[(t + 2) % 3], right[t])
                east = jnp.where(last_lane, left[(t + 1) % 3], left[t])
                spread = northern[t] + southern[t] + (west + east) - 4.0 * centre[t]
                d_row = w_ref[80 * t + row + STEPS : 80 * t + row + STEPS + 1, :]
                new = centre[t] + d_row * spread - winds[t] * (centre[t] - west)
                if final:
                    at = 16 * ((row - skip - TURN) % ROWS) + 8 * t
                    out_ref[at : at + 8, :] = new
                else:
                    at = 24 * row + 8 * t
                    dst[at : at + 8, :] = new
            northern, centre = centre, southern


def analysis_kernel(x_ref, slots_ref, out_ref, pert_ref):
    members = MEMBERS
    both = 2 * members
    tile = (8, PATCH)
    lanes = lax.broadcasted_iota(jnp.int32, tile, 1)
    sub_id = lax.broadcasted_iota(jnp.int32, tile, 0)
    left = lanes < members
    site = slots_ref[4:6, :].astype(jnp.int32)
    level = site // PATCH
    column = site - level * PATCH
    perts, weighteds, forcings = [], [], []
    for p in range(2):
        pick = jnp.broadcast_to(column[p : p + 1, :], (members, PATCH))
        got = None
        for l in range(LEVELS):
            block = x_ref[pl.ds(8 * p + l, members, stride=16), :]
            here = jnp.take_along_axis(block, pick, axis=1, mode="promise_in_bounds")
            got = here if got is None else jnp.where(level[p : p + 1, :] == l, here, got)
        mean = jnp.sum(got, axis=0, keepdims=True) * (1.0 / members)
        pert = got - mean
        weighted = pert * slots_ref[2 + p : 3 + p, :]
        perts.append(pert)
        weighteds.append(weighted)
        innovation = slots_ref[p : p + 1, :] - mean
        forcings.append(jnp.sum(weighted * innovation, axis=1, keepdims=True))
    nt = (((1,), (1,)), ((), ()))
    zero = jnp.zeros((members, PATCH), jnp.float32)
    pair = jnp.concatenate(
        [jnp.concatenate([perts[0], zero], 1), jnp.concatenate([zero, perts[1]], 1)], 0
    )
    cross = lax.dot_general(
        jnp.concatenate(weighteds, 1), pair, nt,
        precision=HIGHEST, preferred_element_type=jnp.float32,
    )
    row_id = lax.broadcasted_iota(jnp.int32, (members, PATCH), 0)
    col_id = lax.broadcasted_iota(jnp.int32, (members, PATCH), 1)
    left_all = col_id < members
    on_diagonal = row_id == col_id - jnp.where(left_all, 0, members)
    m = cross + jnp.where(on_diagonal, members - 1.0, 0.0)
    system = jnp.concatenate([jnp.where(left_all, m, 0.0), jnp.where(left_all, 0.0, m)], 0)
    means = [[None] * LEVELS for _ in range(2)]
    moved = []

    def spread_steps():
        def mm(a, b):
            return jnp.dot(a, b, precision=HIGHEST, preferred_element_type=jnp.float32)

        def centre(l):
            for p in range(2):
                block = x_ref[pl.ds(8 * p + l, members, stride=16), :]
                mean = jnp.sum(block, axis=0, keepdims=True) * (1.0 / members)
                means[p][l] = mean
                pert_ref[p * members : (p + 1) * members, l * PATCH : (l + 1) * PATCH] = block - mean

        squares = jnp.sum(system * system, axis=1, keepdims=True)
        norms = [
            jnp.sqrt(jnp.sum(squares[p * members : (p + 1) * members], axis=0, keepdims=True))
            for p in range(2)
        ]
        first_half = lax.broadcasted_iota(jnp.int32, (both, 1), 0) < members
        norm = jnp.where(first_half, norms[0], norms[1])
        eye = (
            lax.broadcasted_iota(jnp.int32, (both, both), 0)
            == lax.broadcasted_iota(jnp.int32, (both, both), 1)
        ).astype(jnp.float32)
        iterate = system / norm
        root = update = 1.5 * eye - 0.5 * iterate
        for sweep in range(1, NS_ITERS):
            iterate = mm(iterate, update)
            centre(3 * sweep - 3)
            yield
            update = 1.5 * eye - 0.5 * mm(root, iterate)
            centre(3 * sweep - 2)
            yield
            root = mm(update, root)
            if 3 * sweep - 1 < LEVELS:
                centre(3 * sweep - 1)
            yield
        spread = root * jnp.sqrt((members - 1.0) / norm)
        tn = (((0,), (0,)), ((), ()))
        for l in range(LEVELS):
            moved.append(
                lax.dot_general(
                    spread, pert_ref[:, l * PATCH : (l + 1) * PATCH], tn,
                    precision=HIGHEST, preferred_element_type=jnp.float32,
                )
            )
            yield

    m = [m[8 * q : 8 * q + 8, :] for q in range(8)]
    f = [
        jnp.where(left, forcings[0][8 * q : 8 * q + 8, :], forcings[1][8 * q : 8 * q + 8, :])
        for q in range(8)
    ]
    inverse = [[None] * 4 for _ in range(8)]
    steps = spread_steps()

    def spread_row(v, row):
        return jnp.broadcast_to(v[row : row + 1, :], tile)

    for k in range(0, members, 4):
        next(steps, None)
        q, r = divmod(k, 8)
        c = [
            [jnp.take_along_axis(v, jnp.where(left, j, members + j), axis=1, mode="promise_in_bounds") for v in m]
            for j in range(k, k + 4)
        ]
        b = [[spread_row(c[j][q], r + i) for j in range(4)] for i in range(4)]
        det = 1.0 / (b[0][0] * b[1][1] - b[0][1] * b[0][1])
        a00, a01, a11 = b[1][1] * det, -b[0][1] * det, b[0][0] * det
        e00, e01 = a00 * b[0][2] + a01 * b[1][2], a00 * b[0][3] + a01 * b[1][3]
        e10, e11 = a01 * b[0][2] + a11 * b[1][2], a01 * b[0][3] + a11 * b[1][3]
        s00 = b[2][2] - (b[0][2] * e00 + b[1][2] * e10)
        s01 = b[2][3] - (b[0][2] * e01 + b[1][2] * e11)
        s11 = b[3][3] - (b[0][3] * e01 + b[1][3] * e11)
        det = 1.0 / (s00 * s11 - s01 * s01)
        t00, t01, t11 = s11 * det, -s01 * det, s00 * det
        g00, g01 = e00 * t00 + e01 * t01, e00 * t01 + e01 * t11
        g10, g11 = e10 * t00 + e11 * t01, e10 * t01 + e11 * t11
        x01 = a01 + (g00 * e10 + g01 * e11)
        x = [
            [a00 + (g00 * e00 + g01 * e01), x01, -g00, -g01],
            [x01, a11 + (g10 * e10 + g11 * e11), -g10, -g11],
            [-g00, -g10, t00, t01],
            [-g01, -g11, t01, t11],
        ]
        rows = [spread_row(m[q], r + i) for i in range(4)]
        loads = [spread_row(f[q], r + i) for i in range(4)]
        for j in range(4):
            for i in range(4):
                old = inverse[q][j]
                inverse[q][j] = x[i][j] if old is None else jnp.where(sub_id == r + i, x[i][j], old)
        rows = [(x[i][0] * rows[0] + x[i][1] * rows[1]) + (x[i][2] * rows[2] + x[i][3] * rows[3]) for i in range(4)]
        loads = [(x[i][0] * loads[0] + x[i][1] * loads[1]) + (x[i][2] * loads[2] + x[i][3] * loads[3]) for i in range(4)]
        pivot = (sub_id >= r) & (sub_id < r + 4)
        for i in range(4):
            c[i][q] = jnp.where(pivot, 0.0, c[i][q])
        if k < members - 4:
            m = [
                m[n] - ((c[0][n] * rows[0] + c[1][n] * rows[1]) + (c[2][n] * rows[2] + c[3][n] * rows[3]))
                for n in range(8)
            ]
        f = [
            f[n] - ((c[0][n] * loads[0] + c[1][n] * loads[1]) + (c[2][n] * loads[2] + c[3][n] * loads[3]))
            for n in range(8)
        ]
    for _ in steps:
        pass
    weight = []
    for q in range(8):
        terms = [
            inverse[q][j] * jnp.where(sub_id < 4, f[q][j : j + 1, :], f[q][4 + j : 5 + j, :])
            for j in range(4)
        ]
        weight.append((terms[0] + terms[1]) + (terms[2] + terms[3]))
    weight = jnp.concatenate(weight, 0)
    turned = pltpu.roll(weight, members, 1)
    for p in range(2):
        wide = jnp.where(left_all, weight, turned) if p == 0 else jnp.where(left_all, turned, weight)
        for l in range(LEVELS):
            rows = slice(p * members, (p + 1) * members)
            shift = jnp.sum(wide * pert_ref[rows, l * PATCH : (l + 1) * PATCH], axis=0, keepdims=True)
            out_ref[pl.ds(8 * p + l, members, stride=16), :] = moved[l][rows] + (means[p][l] + shift)


def unpack_kernel(x_ref, out_hbm, out_ref, sems):
    copies = []
    for l in range(LEVELS):
        rows = slice(ROWS * l, ROWS * (l + 1))
        for h in range(2):
            cols = slice(h * PATCH, (h + 1) * PATCH)
            base = 8 * h + l
            if TURN:
                out_ref[rows.start : rows.start + TURN, cols] = x_ref[
                    pl.ds(16 * (ROWS - TURN) + base, TURN, stride=16), :
                ]
            out_ref[rows.start + TURN : rows.stop, cols] = x_ref[pl.ds(base, ROWS - TURN, stride=16), :]
        if l % 2:
            some = pl.ds(ROWS * (l - 1), 2 * ROWS)
            copies.append(pltpu.make_async_copy(out_ref.at[some], out_hbm.at[some], sems.at[l // 2]))
            copies[-1].start()
    for copy in copies:
        copy.wait()


VMEM = pl.BlockSpec(memory_space=pltpu.VMEM)
SMEM = pl.BlockSpec(memory_space=pltpu.SMEM)
HBM = pl.BlockSpec(memory_space=pltpu.HBM)


def f32(*dims):
    return jax.ShapeDtypeStruct(dims, jnp.float32)


def call(kernel, outs, specs, scratch=(), flops=1_000_000, name=None, to=VMEM):
    return pl.pallas_call(
        kernel,
        out_shape=outs if len(outs) > 1 else outs[0],
        in_specs=specs,
        out_specs=[to] * len(outs) if len(outs) > 1 else to,
        scratch_shapes=scratch,
        compiler_params=pltpu.CompilerParams(vmem_limit_bytes=VMEM_LIMIT),
        cost_estimate=pl.CostEstimate(flops=flops, bytes_accessed=1_000_000, transcendentals=0),
        name=name,
    )


def exchange(x):
    z, inner = lax.axis_size("grp_0") * lax.axis_size("grp_1"), lax.axis_size("sub") * lax.axis_size("rep")
    groups = [[(g + TURN) % z * inner + i for g in range(z)] for i in range(inner)]
    return lax.all_to_all(x, ("grp_0", "grp_1", "sub", "rep"), 0, 0, axis_index_groups=groups, tiled=True)


def on_device(start, diffusivity, stability, observed, variance, site, live):
    def vmem(*dims, dtype=jnp.float32):
        return pltpu.VMEM(dims, dtype)

    send = call(
        pack_kernel,
        [f32(2 * SUBS * BLOCK, PATCH)],
        [HBM] * 7,
        scratch=[
            vmem(LEVELS, 8, COLS),
            vmem(LEVELS, 8, COLS),
            vmem(8, COLS),
            vmem(8, COLS),
            vmem(LEVELS, ROWS, PATCH),
            vmem(ROWS, PATCH),
            vmem(1, LEVELS),
            vmem(2, PATCH),
            vmem(2, PATCH),
            vmem(2, PATCH, dtype=jnp.int32),
            vmem(1, 2, dtype=jnp.int32),
            pltpu.SemaphoreType.DMA((11,)),
        ],
        name="pack",
    )(
        *(
            pltpu.with_memory_space_constraint(v, pltpu.HBM)
            for v in (
                start.reshape(LEVELS, ROWS, COLS),
                diffusivity,
                stability,
                observed.reshape(2, PATCH),
                variance.reshape(2, PATCH),
                site.reshape(2, PATCH),
                live,
            )
        )
    )
    got = lax.all_to_all(send.reshape(2 * SUBS, BLOCK, PATCH), ("sub", "rep"), 0, 0, tiled=True)
    forecast, slots = call(
        forecast_kernel,
        [f32(ROWS * 16, PATCH), f32(8, PATCH)],
        [VMEM] * 3,
        scratch=[vmem(24 * TALL, PATCH), vmem(24 * TALL, PATCH), vmem(3 * (ROWS + 16), PATCH)],
        name="forecast",
    )(start.reshape(LEVELS * ROWS, COLS), diffusivity, got.reshape(2 * SUBS * BLOCK, PATCH))
    gathered = exchange(forecast.reshape(ROWS, 16, PATCH))
    analysed = call(
        analysis_kernel,
        [f32(MEMBERS * 16, PATCH)],
        [VMEM] * 2,
        scratch=[pltpu.VMEM((2 * MEMBERS, LEVELS * PATCH), jnp.float32)],
        name="analysis",
    )(gathered.reshape(MEMBERS * 16, PATCH), slots)
    returned = exchange(analysed.reshape(MEMBERS, 16, PATCH))
    out = call(
        unpack_kernel,
        [f32(LEVELS * ROWS, COLS)],
        [VMEM],
        scratch=[vmem(LEVELS * ROWS, COLS), pltpu.SemaphoreType.DMA((LEVELS // 2,))],
        name="unpack",
        to=HBM,
    )(
        returned.reshape(ROWS * 16, PATCH)
    )
    return out.reshape(1, LEVELS, ROWS, COLS)


def solution(mesh):
    split = Mesh(
        mesh.devices.reshape(16, 4, mesh.shape["sub"], mesh.shape["rep"]),
        ("grp_0", "grp_1", "sub", "rep"),
    )
    return jax.shard_map(
        on_device,
        mesh=split,
        in_specs=(
            P(GRP, None, "sub", "rep"),
            P("sub", "rep"),
            P(GRP, None),
            P(SUB_GRP, "rep", None),
            P(SUB_GRP, "rep", None),
            P(SUB_GRP, "rep", None),
            P(SUB_GRP, "rep"),
        ),
        out_specs=P(GRP, None, "sub", "rep"),
        check_vma=False,
    )
```

```python
import jax
import jax.numpy as jnp
from jax import lax
from jax.experimental import pallas as pl
from jax.experimental.pallas import tpu as pltpu
from jax.sharding import Mesh
from jax.sharding import PartitionSpec as P

LEVELS = 8
PATCH = 128
STEPS = 4
NS_ITERS = 4
MEMBERS = 64
ROWS = 64
COLS = 256
TALL = ROWS + 2 * STEPS
GRP = ("grp_0", "grp_1")
SUB_GRP = ("sub", "grp_0", "grp_1")
HIGHEST = lax.Precision.HIGHEST
VMEM_LIMIT = 24 * 1024 * 1024
SUBS = 4
BLOCK = 72
TURN = 46


def block(y, rep):
    return pl.multiple_of(BLOCK * (2 * y + 1 - rep), 8)


def pack_kernel(
    x_ref, d_ref, stability_ref, obs_hbm, var_hbm, site_hbm, count_hbm, send_ref,
    top_ref, end_ref, dtop_ref, dend_ref, edge_ref, dedge_ref, calm_ref, obs_ref, var_ref, site_ref, count_ref, sems,
):
    y, rep = lax.axis_index("sub"), lax.axis_index("rep")
    half = pl.ds(pl.multiple_of((1 - rep) * PATCH, PATCH), PATCH)
    copies = [
        pltpu.make_async_copy(src, dst, sems.at[i])
        for i, (src, dst) in enumerate(
            (
                (x_ref.at[:, :, half], edge_ref),
                (d_ref.at[:, half], dedge_ref),
                (x_ref.at[:, pl.ds(0, 8), :], top_ref),
                (x_ref.at[:, pl.ds(ROWS - 8, 8), :], end_ref),
                (d_ref.at[pl.ds(0, 8), :], dtop_ref),
                (d_ref.at[pl.ds(ROWS - 8, 8), :], dend_ref),
                (stability_ref, calm_ref),
                (obs_hbm, obs_ref),
                (var_hbm, var_ref),
                (site_hbm, site_ref),
                (count_hbm, count_ref),
            )
        )
    ]
    for copy in copies:
        copy.start()
    sub_id = lax.broadcasted_iota(jnp.int32, (8, PATCH), 0)
    lane = lax.broadcasted_iota(jnp.int32, (8, PATCH), 1)
    for copy in copies:
        copy.wait()
    away = lax.rem(y + 2, SUBS)
    side_at = block(y, 1 - rep)
    for l in range(LEVELS + 1):
        packed = jnp.zeros((8, PATCH), jnp.float32)
        for r in range(8):
            rows = slice(8 * r, 8 * r + 8)
            tile = edge_ref[l, rows, :] if l < LEVELS else dedge_ref[rows, :]
            turned = pltpu.roll(tile, lax.rem(16 * (r + 1 - rep), PATCH), 1)
            packed = jnp.where(lane // 16 == r, turned, packed)
        send_ref[pl.ds(side_at + 8 * l, 8), :] = packed
    for ok, step, rows_ref, d_rows, first in (
        (y > 0, -1, top_ref, dtop_ref, 0),
        (y < SUBS - 1, 1, end_ref, dend_ref, 8 - STEPS),
    ):
        there_y = jnp.where(ok, y + step, away)
        at, corner = block(there_y, rep), block(there_y, 1 - rep)
        for l in range(LEVELS):
            send_ref[pl.ds(corner + l, STEPS, stride=8), :] = edge_ref[
                l, (first // 4) * (ROWS - 8) + first : (first // 4) * (ROWS - 8) + first + STEPS, :
            ]
        send_ref[pl.ds(corner + 32, STEPS), :] = dedge_ref[
            (first // 4) * (ROWS - 8) + first : (first // 4) * (ROWS - 8) + first + STEPS, :
        ]
        for h in range(2):
            cols = slice(h * PATCH, (h + 1) * PATCH)
            for l in range(LEVELS):
                send_ref[pl.ds(at + 8 * h + l, STEPS, stride=16), :] = rows_ref[
                    l, first : first + STEPS, cols
                ]
            send_ref[pl.ds(at + 64 + STEPS * h, STEPS), :] = d_rows[first : first + STEPS, cols]
    own = block(y, rep)
    picked = jnp.where(sub_id[:, :8] == lane[:, :8], calm_ref[...], 0.0)
    send_ref[pl.ds(own, 8), :] = jnp.broadcast_to(jnp.sum(picked, axis=1, keepdims=True), (LEVELS, PATCH))
    send_ref[pl.ds(own + 8, 2), :] = obs_ref[...]
    for p in range(2):
        live = lane[:1] < count_ref[:, p : p + 1]
        send_ref[pl.ds(own + 10 + p, 1), :] = jnp.where(live, 1.0 / var_ref[p : p + 1, :], 0.0)
    send_ref[pl.ds(own + 12, 2), :] = site_ref[...].astype(jnp.float32)


def forecast_kernel(x_ref, d_ref, got_ref, out_ref, slots_ref, a_ref, b_ref, w_ref):
    y, rep = lax.axis_index("sub"), lax.axis_index("rep")
    lane = lax.broadcasted_iota(jnp.int32, (8, PATCH), 1)
    low = jnp.where(rep == 0, 0, PATCH - STEPS)
    keep = (lane >= low) & (lane < low + STEPS)
    away = lax.rem(y + 2, SUBS)
    side_at = block(y, 1 - rep)
    own = 24 * STEPS
    for l in range(LEVELS + 1):
        packed = got_ref[pl.ds(side_at + 8 * l, 8), :]
        for r in range(8):
            turned = pltpu.roll(packed, lax.rem(PATCH - 16 * (r + rep), PATCH), 1)
            side = jnp.where(keep, turned, 0.0)
            if l < LEVELS:
                a_ref[pl.ds(own + 24 * 8 * r + 16 + l, 8, stride=24), :] = side
            else:
                w_ref[168 + 8 * r : 176 + 8 * r, :] = side
    for l in range(LEVELS):
        for t in range(2):
            a_ref[pl.ds(own + 8 * t + l, ROWS, stride=24), :] = x_ref[
                ROWS * l : ROWS * (l + 1), t * PATCH : (t + 1) * PATCH
            ]
    for t in range(2):
        w_ref[80 * t + 8 : 80 * t + 8 + ROWS, :] = d_ref[:, t * PATCH : (t + 1) * PATCH]
    for ok, step, base, d_base in (
        (y > 0, -1, 0, STEPS),
        (y < SUBS - 1, 1, STEPS + ROWS, 8 + ROWS),
    ):
        there_y = jnp.where(ok, y + step, away)
        at, corner = block(there_y, rep), block(there_y, 1 - rep)
        there = jnp.broadcast_to(ok, (8, PATCH))
        both = keep & there
        for r in range(STEPS):
            to = 24 * (base + r)
            for t in range(2):
                a_ref[to + 8 * t : to + 8 * t + 8, :] = jnp.where(
                    there, got_ref[pl.ds(at + 16 * r + 8 * t, 8), :], 0.0
                )
            a_ref[to + 16 : to + 24, :] = jnp.where(both, got_ref[pl.ds(corner + 8 * r, 8), :], 0.0)
        rows = jnp.where(there, got_ref[pl.ds(at + 64, 8), :], 0.0)
        for t in range(2):
            w_ref[80 * t + d_base : 80 * t + d_base + STEPS, :] = rows[STEPS * t : STEPS * (t + 1)]
        rows = jnp.where(both, got_ref[pl.ds(corner + 32, 8), :], 0.0)
        w_ref[160 + d_base : 160 + d_base + STEPS, :] = rows[:STEPS]
    mine = block(y, rep)
    wind = got_ref[pl.ds(mine, 8), :]
    slots_ref[...] = got_ref[pl.ds(mine + 8, 8), :]
    winds = [wind, wind, jnp.where(keep, wind, 0.0)]
    first_lane, last_lane = lane == 0, lane == PATCH - 1

    for step in range(STEPS):
        src, dst = (a_ref, b_ref) if step % 2 == 0 else (b_ref, a_ref)
        final = step == STEPS - 1
        skip = STEPS if final else step + 1

        def tiles(row):
            return [src[24 * row + 8 * t : 24 * row + 8 * t + 8, :] for t in range(3)]

        northern, centre = tiles(skip - 1), tiles(skip)
        for row in range(skip, TALL - skip):
            southern = tiles(row + 1)
            right = [pltpu.roll(v, 1, 1) for v in centre]
            left = [pltpu.roll(v, PATCH - 1, 1) for v in centre]
            for t in range(2 if final else 3):
                west = jnp.where(first_lane, right[(t + 2) % 3], right[t])
                east = jnp.where(last_lane, left[(t + 1) % 3], left[t])
                spread = northern[t] + southern[t] + (west + east) - 4.0 * centre[t]
                d_row = w_ref[80 * t + row + STEPS : 80 * t + row + STEPS + 1, :]
                new = centre[t] + d_row * spread - winds[t] * (centre[t] - west)
                if final:
                    at = 16 * ((row - skip - TURN) % ROWS) + 8 * t
                    out_ref[at : at + 8, :] = new
                else:
                    at = 24 * row + 8 * t
                    dst[at : at + 8, :] = new
            northern, centre = centre, southern


def analysis_kernel(x_ref, slots_ref, out_ref, pert_ref):
    members = MEMBERS
    both = 2 * members
    tile = (8, PATCH)
    lanes = lax.broadcasted_iota(jnp.int32, tile, 1)
    sub_id = lax.broadcasted_iota(jnp.int32, tile, 0)
    left = lanes < members
    site = slots_ref[4:6, :].astype(jnp.int32)
    level = site // PATCH
    column = site - level * PATCH
    perts, weighteds, forcings = [], [], []
    for p in range(2):
        pick = jnp.broadcast_to(column[p : p + 1, :], (members, PATCH))
        got = None
        for l in range(LEVELS):
            block = x_ref[pl.ds(8 * p + l, members, stride=16), :]
            here = jnp.take_along_axis(block, pick, axis=1, mode="promise_in_bounds")
            got = here if got is None else jnp.where(level[p : p + 1, :] == l, here, got)
        mean = jnp.sum(got, axis=0, keepdims=True) * (1.0 / members)
        pert = got - mean
        weighted = pert * slots_ref[2 + p : 3 + p, :]
        perts.append(pert)
        weighteds.append(weighted)
        innovation = slots_ref[p : p + 1, :] - mean
        forcings.append(jnp.sum(weighted * innovation, axis=1, keepdims=True))
    nt = (((1,), (1,)), ((), ()))
    zero = jnp.zeros((members, PATCH), jnp.float32)
    pair = jnp.concatenate(
        [jnp.concatenate([perts[0], zero], 1), jnp.concatenate([zero, perts[1]], 1)], 0
    )
    cross = lax.dot_general(
        jnp.concatenate(weighteds, 1), pair, nt,
        precision=HIGHEST, preferred_element_type=jnp.float32,
    )
    row_id = lax.broadcasted_iota(jnp.int32, (members, PATCH), 0)
    col_id = lax.broadcasted_iota(jnp.int32, (members, PATCH), 1)
    left_all = col_id < members
    on_diagonal = row_id == col_id - jnp.where(left_all, 0, members)
    m = cross + jnp.where(on_diagonal, members - 1.0, 0.0)
    system = jnp.concatenate([jnp.where(left_all, m, 0.0), jnp.where(left_all, 0.0, m)], 0)
    means = [[None] * LEVELS for _ in range(2)]
    moved = []

    def spread_steps():
        def mm(a, b):
            return jnp.dot(a, b, precision=HIGHEST, preferred_element_type=jnp.float32)

        def centre(l):
            for p in range(2):
                block = x_ref[pl.ds(8 * p + l, members, stride=16), :]
                mean = jnp.sum(block, axis=0, keepdims=True) * (1.0 / members)
                means[p][l] = mean
                pert_ref[p * members : (p + 1) * members, l * PATCH : (l + 1) * PATCH] = block - mean

        squares = jnp.sum(system * system, axis=1, keepdims=True)
        norms = [
            jnp.sqrt(jnp.sum(squares[p * members : (p + 1) * members], axis=0, keepdims=True))
            for p in range(2)
        ]
        first_half = lax.broadcasted_iota(jnp.int32, (both, 1), 0) < members
        norm = jnp.where(first_half, norms[0], norms[1])
        eye = (
            lax.broadcasted_iota(jnp.int32, (both, both), 0)
            == lax.broadcasted_iota(jnp.int32, (both, both), 1)
        ).astype(jnp.float32)
        iterate = system / norm
        root = update = 1.5 * eye - 0.5 * iterate
        for sweep in range(1, NS_ITERS):
            iterate = mm(iterate, update)
            centre(3 * sweep - 3)
            yield
            update = 1.5 * eye - 0.5 * mm(root, iterate)
            centre(3 * sweep - 2)
            yield
            root = mm(update, root)
            if 3 * sweep - 1 < LEVELS:
                centre(3 * sweep - 1)
            yield
        spread = root * jnp.sqrt((members - 1.0) / norm)
        tn = (((0,), (0,)), ((), ()))
        for l in range(LEVELS):
            moved.append(
                lax.dot_general(
                    spread, pert_ref[:, l * PATCH : (l + 1) * PATCH], tn,
                    precision=HIGHEST, preferred_element_type=jnp.float32,
                )
            )
            yield

    m = [m[8 * q : 8 * q + 8, :] for q in range(8)]
    f = [
        jnp.where(left, forcings[0][8 * q : 8 * q + 8, :], forcings[1][8 * q : 8 * q + 8, :])
        for q in range(8)
    ]
    inverse = [[None] * 4 for _ in range(8)]
    steps = spread_steps()

    def spread_row(v, row):
        return jnp.broadcast_to(v[row : row + 1, :], tile)

    for k in range(0, members, 4):
        next(steps, None)
        q, r = divmod(k, 8)
        c = [
            [jnp.take_along_axis(v, jnp.where(left, j, members + j), axis=1, mode="promise_in_bounds") for v in m]
            for j in range(k, k + 4)
        ]
        b = [[spread_row(c[j][q], r + i) for j in range(4)] for i in range(4)]
        det = 1.0 / (b[0][0] * b[1][1] - b[0][1] * b[0][1])
        a00, a01, a11 = b[1][1] * det, -b[0][1] * det, b[0][0] * det
        e00, e01 = a00 * b[0][2] + a01 * b[1][2], a00 * b[0][3] + a01 * b[1][3]
        e10, e11 = a01 * b[0][2] + a11 * b[1][2], a01 * b[0][3] + a11 * b[1][3]
        s00 = b[2][2] - (b[0][2] * e00 + b[1][2] * e10)
        s01 = b[2][3] - (b[0][2] * e01 + b[1][2] * e11)
        s11 = b[3][3] - (b[0][3] * e01 + b[1][3] * e11)
        det = 1.0 / (s00 * s11 - s01 * s01)
        t00, t01, t11 = s11 * det, -s01 * det, s00 * det
        g00, g01 = e00 * t00 + e01 * t01, e00 * t01 + e01 * t11
        g10, g11 = e10 * t00 + e11 * t01, e10 * t01 + e11 * t11
        x01 = a01 + (g00 * e10 + g01 * e11)
        x = [
            [a00 + (g00 * e00 + g01 * e01), x01, -g00, -g01],
            [x01, a11 + (g10 * e10 + g11 * e11), -g10, -g11],
            [-g00, -g10, t00, t01],
            [-g01, -g11, t01, t11],
        ]
        rows = [spread_row(m[q], r + i) for i in range(4)]
        loads = [spread_row(f[q], r + i) for i in range(4)]
        for j in range(4):
            for i in range(4):
                old = inverse[q][j]
                inverse[q][j] = x[i][j] if old is None else jnp.where(sub_id == r + i, x[i][j], old)
        rows = [(x[i][0] * rows[0] + x[i][1] * rows[1]) + (x[i][2] * rows[2] + x[i][3] * rows[3]) for i in range(4)]
        loads = [(x[i][0] * loads[0] + x[i][1] * loads[1]) + (x[i][2] * loads[2] + x[i][3] * loads[3]) for i in range(4)]
        pivot = (sub_id >= r) & (sub_id < r + 4)
        for i in range(4):
            c[i][q] = jnp.where(pivot, 0.0, c[i][q])
        if k < members - 4:
            m = [
                m[n] - ((c[0][n] * rows[0] + c[1][n] * rows[1]) + (c[2][n] * rows[2] + c[3][n] * rows[3]))
                for n in range(8)
            ]
        f = [
            f[n] - ((c[0][n] * loads[0] + c[1][n] * loads[1]) + (c[2][n] * loads[2] + c[3][n] * loads[3]))
            for n in range(8)
        ]
    for _ in steps:
        pass
    weight = []
    for q in range(8):
        terms = [
            inverse[q][j] * jnp.where(sub_id < 4, f[q][j : j + 1, :], f[q][4 + j : 5 + j, :])
            for j in range(4)
        ]
        weight.append((terms[0] + terms[1]) + (terms[2] + terms[3]))
    weight = jnp.concatenate(weight, 0)
    turned = pltpu.roll(weight, members, 1)
    for p in range(2):
        wide = jnp.where(left_all, weight, turned) if p == 0 else jnp.where(left_all, turned, weight)
        for l in range(LEVELS):
            rows = slice(p * members, (p + 1) * members)
            shift = jnp.sum(wide * pert_ref[rows, l * PATCH : (l + 1) * PATCH], axis=0, keepdims=True)
            out_ref[pl.ds(8 * p + l, members, stride=16), :] = moved[l][rows] + (means[p][l] + shift)


def unpack_kernel(x_ref, out_hbm, out_ref, sems):
    copies = []
    for l in range(LEVELS):
        rows = slice(ROWS * l, ROWS * (l + 1))
        for h in range(2):
            cols = slice(h * PATCH, (h + 1) * PATCH)
            base = 8 * h + l
            if TURN:
                out_ref[rows.start : rows.start + TURN, cols] = x_ref[
                    pl.ds(16 * (ROWS - TURN) + base, TURN, stride=16), :
                ]
            out_ref[rows.start + TURN : rows.stop, cols] = x_ref[pl.ds(base, ROWS - TURN, stride=16), :]
        if l % 2:
            some = pl.ds(ROWS * (l - 1), 2 * ROWS)
            copies.append(pltpu.make_async_copy(out_ref.at[some], out_hbm.at[some], sems.at[l // 2]))
            copies[-1].start()
    for copy in copies:
        copy.wait()


VMEM = pl.BlockSpec(memory_space=pltpu.VMEM)
SMEM = pl.BlockSpec(memory_space=pltpu.SMEM)
HBM = pl.BlockSpec(memory_space=pltpu.HBM)


def f32(*dims):
    return jax.ShapeDtypeStruct(dims, jnp.float32)


def call(kernel, outs, specs, scratch=(), flops=1_000_000, name=None, to=VMEM):
    return pl.pallas_call(
        kernel,
        out_shape=outs if len(outs) > 1 else outs[0],
        in_specs=specs,
        out_specs=[to] * len(outs) if len(outs) > 1 else to,
        scratch_shapes=scratch,
        compiler_params=pltpu.CompilerParams(vmem_limit_bytes=VMEM_LIMIT),
        cost_estimate=pl.CostEstimate(flops=flops, bytes_accessed=1_000_000, transcendentals=0),
        name=name,
    )


def exchange(x):
    z, inner = lax.axis_size("grp_0") * lax.axis_size("grp_1"), lax.axis_size("sub") * lax.axis_size("rep")
    groups = [[(g + TURN) % z * inner + i for g in range(z)] for i in range(inner)]
    return lax.all_to_all(x, ("grp_0", "grp_1", "sub", "rep"), 0, 0, axis_index_groups=groups, tiled=True)


def swap_ends(x):
    grp = lax.axis_size("grp_0") * lax.axis_size("grp_1")
    groups = [[2 * (SUBS * g + y) + rep for y in range(SUBS) for rep in (1, 0)] for g in range(grp)]
    return lax.all_to_all(x, ("grp_0", "grp_1", "sub", "rep"), 0, 0, axis_index_groups=groups, tiled=True)


def on_device(start, diffusivity, stability, observed, variance, site, live):
    def vmem(*dims, dtype=jnp.float32):
        return pltpu.VMEM(dims, dtype)

    send = call(
        pack_kernel,
        [f32(2 * SUBS * BLOCK, PATCH)],
        [HBM] * 7,
        scratch=[
            vmem(LEVELS, 8, COLS),
            vmem(LEVELS, 8, COLS),
            vmem(8, COLS),
            vmem(8, COLS),
            vmem(LEVELS, ROWS, PATCH),
            vmem(ROWS, PATCH),
            vmem(1, LEVELS),
            vmem(2, PATCH),
            vmem(2, PATCH),
            vmem(2, PATCH, dtype=jnp.int32),
            vmem(1, 2, dtype=jnp.int32),
            pltpu.SemaphoreType.DMA((11,)),
        ],
        name="pack",
    )(
        *(
            pltpu.with_memory_space_constraint(v, pltpu.HBM)
            for v in (
                start.reshape(LEVELS, ROWS, COLS),
                diffusivity,
                stability,
                observed.reshape(2, PATCH),
                variance.reshape(2, PATCH),
                site.reshape(2, PATCH),
                live,
            )
        )
    )
    got = swap_ends(send.reshape(2 * SUBS, BLOCK, PATCH))
    forecast, slots = call(
        forecast_kernel,
        [f32(ROWS * 16, PATCH), f32(8, PATCH)],
        [VMEM] * 3,
        scratch=[vmem(24 * TALL, PATCH), vmem(24 * TALL, PATCH), vmem(3 * (ROWS + 16), PATCH)],
        name="forecast",
    )(start.reshape(LEVELS * ROWS, COLS), diffusivity, got.reshape(2 * SUBS * BLOCK, PATCH))
    gathered = exchange(forecast.reshape(ROWS, 16, PATCH))
    analysed = call(
        analysis_kernel,
        [f32(MEMBERS * 16, PATCH)],
        [VMEM] * 2,
        scratch=[pltpu.VMEM((2 * MEMBERS, LEVELS * PATCH), jnp.float32)],
        name="analysis",
    )(gathered.reshape(MEMBERS * 16, PATCH), slots)
    returned = exchange(analysed.reshape(MEMBERS, 16, PATCH))
    out = call(
        unpack_kernel,
        [f32(LEVELS * ROWS, COLS)],
        [VMEM],
        scratch=[vmem(LEVELS * ROWS, COLS), pltpu.SemaphoreType.DMA((LEVELS // 2,))],
        name="unpack",
        to=HBM,
    )(
        returned.reshape(ROWS * 16, PATCH)
    )
    return out.reshape(1, LEVELS, ROWS, COLS)


def solution(mesh):
    split = Mesh(
        mesh.devices.reshape(16, 4, mesh.shape["sub"], mesh.shape["rep"]),
        ("grp_0", "grp_1", "sub", "rep"),
    )
    return jax.shard_map(
        on_device,
        mesh=split,
        in_specs=(
            P(GRP, None, "sub", "rep"),
            P("sub", "rep"),
            P(GRP, None),
            P(SUB_GRP, "rep", None),
            P(SUB_GRP, "rep", None),
            P(SUB_GRP, "rep", None),
            P(SUB_GRP, "rep"),
        ),
        out_specs=P(GRP, None, "sub", "rep"),
        check_vma=False,
    )
```

```python
import jax
import jax.numpy as jnp
from jax import lax
from jax.experimental import pallas as pl
from jax.experimental.pallas import tpu as pltpu
from jax.sharding import Mesh
from jax.sharding import PartitionSpec as P

LEVELS = 8
PATCH = 128
STEPS = 4
NS_ITERS = 4
MEMBERS = 64
ROWS = 64
COLS = 256
TALL = ROWS + 2 * STEPS
GRP = ("grp_0", "grp_1")
SUB_GRP = ("sub", "grp_0", "grp_1")
HIGHEST = lax.Precision.HIGHEST
VMEM_LIMIT = 24 * 1024 * 1024
SUBS = 4
BLOCK = 72
TURN = 46


def block(y, rep):
    return pl.multiple_of(BLOCK * (2 * y + 1 - rep), 8)


def pack_kernel(
    x_ref, d_ref, stability_ref, obs_hbm, var_hbm, site_hbm, count_hbm, send_ref,
    top_ref, end_ref, dtop_ref, dend_ref, edge_ref, dedge_ref, calm_ref, obs_ref, var_ref, site_ref, count_ref, sems,
):
    y, rep = lax.axis_index("sub"), lax.axis_index("rep")
    half = pl.ds(pl.multiple_of((1 - rep) * PATCH, PATCH), PATCH)
    copies = [
        pltpu.make_async_copy(src, dst, sems.at[i])
        for i, (src, dst) in enumerate(
            (
                (x_ref.at[:, :, half], edge_ref),
                (d_ref.at[:, half], dedge_ref),
                (x_ref.at[:, pl.ds(0, 8), :], top_ref),
                (x_ref.at[:, pl.ds(ROWS - 8, 8), :], end_ref),
                (d_ref.at[pl.ds(0, 8), :], dtop_ref),
                (d_ref.at[pl.ds(ROWS - 8, 8), :], dend_ref),
                (stability_ref, calm_ref),
                (obs_hbm, obs_ref),
                (var_hbm, var_ref),
                (site_hbm, site_ref),
                (count_hbm, count_ref),
            )
        )
    ]
    for copy in copies:
        copy.start()
    sub_id = lax.broadcasted_iota(jnp.int32, (8, PATCH), 0)
    lane = lax.broadcasted_iota(jnp.int32, (8, PATCH), 1)
    for copy in copies[:2]:
        copy.wait()
    away = lax.rem(y + 2, SUBS)
    side_at = block(y, 1 - rep)
    for l in range(LEVELS + 1):
        packed = jnp.zeros((8, PATCH), jnp.float32)
        for r in range(8):
            rows = slice(8 * r, 8 * r + 8)
            tile = edge_ref[l, rows, :] if l < LEVELS else dedge_ref[rows, :]
            turned = pltpu.roll(tile, lax.rem(16 * (r + 1 - rep), PATCH), 1)
            packed = jnp.where(lane // 16 == r, turned, packed)
        send_ref[pl.ds(side_at + 8 * l, 8), :] = packed
    for copy in copies[2:6]:
        copy.wait()
    for ok, step, rows_ref, d_rows, first in (
        (y > 0, -1, top_ref, dtop_ref, 0),
        (y < SUBS - 1, 1, end_ref, dend_ref, 8 - STEPS),
    ):
        there_y = jnp.where(ok, y + step, away)
        at, corner = block(there_y, rep), block(there_y, 1 - rep)
        for l in range(LEVELS):
            send_ref[pl.ds(corner + l, STEPS, stride=8), :] = edge_ref[
                l, (first // 4) * (ROWS - 8) + first : (first // 4) * (ROWS - 8) + first + STEPS, :
            ]
        send_ref[pl.ds(corner + 32, STEPS), :] = dedge_ref[
            (first // 4) * (ROWS - 8) + first : (first // 4) * (ROWS - 8) + first + STEPS, :
        ]
        for h in range(2):
            cols = slice(h * PATCH, (h + 1) * PATCH)
            for l in range(LEVELS):
                send_ref[pl.ds(at + 8 * h + l, STEPS, stride=16), :] = rows_ref[
                    l, first : first + STEPS, cols
                ]
            send_ref[pl.ds(at + 64 + STEPS * h, STEPS), :] = d_rows[first : first + STEPS, cols]
    for copy in copies[6:]:
        copy.wait()
    own = block(y, rep)
    picked = jnp.where(sub_id[:, :8] == lane[:, :8], calm_ref[...], 0.0)
    send_ref[pl.ds(own, 8), :] = jnp.broadcast_to(jnp.sum(picked, axis=1, keepdims=True), (LEVELS, PATCH))
    send_ref[pl.ds(own + 8, 2), :] = obs_ref[...]
    for p in range(2):
        live = lane[:1] < count_ref[:, p : p + 1]
        send_ref[pl.ds(own + 10 + p, 1), :] = jnp.where(live, 1.0 / var_ref[p : p + 1, :], 0.0)
    send_ref[pl.ds(own + 12, 2), :] = site_ref[...].astype(jnp.float32)


def forecast_kernel(x_ref, d_ref, got_ref, out_ref, slots_ref, a_ref, b_ref, w_ref):
    y, rep = lax.axis_index("sub"), lax.axis_index("rep")
    lane = lax.broadcasted_iota(jnp.int32, (8, PATCH), 1)
    low = jnp.where(rep == 0, 0, PATCH - STEPS)
    keep = (lane >= low) & (lane < low + STEPS)
    away = lax.rem(y + 2, SUBS)
    side_at = block(y, 1 - rep)
    own = 24 * STEPS
    for l in range(LEVELS + 1):
        packed = got_ref[pl.ds(side_at + 8 * l, 8), :]
        for r in range(8):
            turned = pltpu.roll(packed, lax.rem(PATCH - 16 * (r + rep), PATCH), 1)
            side = jnp.where(keep, turned, 0.0)
            if l < LEVELS:
                a_ref[pl.ds(own + 24 * 8 * r + 16 + l, 8, stride=24), :] = side
            else:
                w_ref[168 + 8 * r : 176 + 8 * r, :] = side
    for l in range(LEVELS):
        for t in range(2):
            a_ref[pl.ds(own + 8 * t + l, ROWS, stride=24), :] = x_ref[
                ROWS * l : ROWS * (l + 1), t * PATCH : (t + 1) * PATCH
            ]
    for t in range(2):
        w_ref[80 * t + 8 : 80 * t + 8 + ROWS, :] = d_ref[:, t * PATCH : (t + 1) * PATCH]
    for ok, step, base, d_base in (
        (y > 0, -1, 0, STEPS),
        (y < SUBS - 1, 1, STEPS + ROWS, 8 + ROWS),
    ):
        there_y = jnp.where(ok, y + step, away)
        at, corner = block(there_y, rep), block(there_y, 1 - rep)
        there = jnp.broadcast_to(ok, (8, PATCH))
        both = keep & there
        for r in range(STEPS):
            to = 24 * (base + r)
            for t in range(2):
                a_ref[to + 8 * t : to + 8 * t + 8, :] = jnp.where(
                    there, got_ref[pl.ds(at + 16 * r + 8 * t, 8), :], 0.0
                )
            a_ref[to + 16 : to + 24, :] = jnp.where(both, got_ref[pl.ds(corner + 8 * r, 8), :], 0.0)
        rows = jnp.where(there, got_ref[pl.ds(at + 64, 8), :], 0.0)
        for t in range(2):
            w_ref[80 * t + d_base : 80 * t + d_base + STEPS, :] = rows[STEPS * t : STEPS * (t + 1)]
        rows = jnp.where(both, got_ref[pl.ds(corner + 32, 8), :], 0.0)
        w_ref[160 + d_base : 160 + d_base + STEPS, :] = rows[:STEPS]
    mine = block(y, rep)
    wind = got_ref[pl.ds(mine, 8), :]
    slots_ref[...] = got_ref[pl.ds(mine + 8, 8), :]
    winds = [wind, wind, jnp.where(keep, wind, 0.0)]
    first_lane, last_lane = lane == 0, lane == PATCH - 1

    for step in range(STEPS):
        src, dst = (a_ref, b_ref) if step % 2 == 0 else (b_ref, a_ref)
        final = step == STEPS - 1
        skip = STEPS if final else step + 1

        def tiles(row):
            return [src[24 * row + 8 * t : 24 * row + 8 * t + 8, :] for t in range(3)]

        northern, centre = tiles(skip - 1), tiles(skip)
        for row in range(skip, TALL - skip):
            southern = tiles(row + 1)
            right = [pltpu.roll(v, 1, 1) for v in centre]
            left = [pltpu.roll(v, PATCH - 1, 1) for v in centre]
            for t in range(2 if final else 3):
                west = jnp.where(first_lane, right[(t + 2) % 3], right[t])
                east = jnp.where(last_lane, left[(t + 1) % 3], left[t])
                spread = northern[t] + southern[t] + (west + east) - 4.0 * centre[t]
                d_row = w_ref[80 * t + row + STEPS : 80 * t + row + STEPS + 1, :]
                new = centre[t] + d_row * spread - winds[t] * (centre[t] - west)
                if final:
                    at = 16 * ((row - skip - TURN) % ROWS) + 8 * t
                    out_ref[at : at + 8, :] = new
                else:
                    at = 24 * row + 8 * t
                    dst[at : at + 8, :] = new
            northern, centre = centre, southern


def analysis_kernel(x_ref, slots_ref, out_ref, pert_ref):
    members = MEMBERS
    both = 2 * members
    tile = (8, PATCH)
    lanes = lax.broadcasted_iota(jnp.int32, tile, 1)
    sub_id = lax.broadcasted_iota(jnp.int32, tile, 0)
    left = lanes < members
    site = slots_ref[4:6, :].astype(jnp.int32)
    level = site // PATCH
    column = site - level * PATCH
    perts, weighteds, forcings = [], [], []
    for p in range(2):
        pick = jnp.broadcast_to(column[p : p + 1, :], (members, PATCH))
        got = None
        for l in range(LEVELS):
            block = x_ref[pl.ds(8 * p + l, members, stride=16), :]
            here = jnp.take_along_axis(block, pick, axis=1, mode="promise_in_bounds")
            got = here if got is None else jnp.where(level[p : p + 1, :] == l, here, got)
        mean = jnp.sum(got, axis=0, keepdims=True) * (1.0 / members)
        pert = got - mean
        weighted = pert * slots_ref[2 + p : 3 + p, :]
        perts.append(pert)
        weighteds.append(weighted)
        innovation = slots_ref[p : p + 1, :] - mean
        forcings.append(jnp.sum(weighted * innovation, axis=1, keepdims=True))
    nt = (((1,), (1,)), ((), ()))
    zero = jnp.zeros((members, PATCH), jnp.float32)
    pair = jnp.concatenate(
        [jnp.concatenate([perts[0], zero], 1), jnp.concatenate([zero, perts[1]], 1)], 0
    )
    cross = lax.dot_general(
        jnp.concatenate(weighteds, 1), pair, nt,
        precision=HIGHEST, preferred_element_type=jnp.float32,
    )
    row_id = lax.broadcasted_iota(jnp.int32, (members, PATCH), 0)
    col_id = lax.broadcasted_iota(jnp.int32, (members, PATCH), 1)
    left_all = col_id < members
    on_diagonal = row_id == col_id - jnp.where(left_all, 0, members)
    m = cross + jnp.where(on_diagonal, members - 1.0, 0.0)
    system = jnp.concatenate([jnp.where(left_all, m, 0.0), jnp.where(left_all, 0.0, m)], 0)
    means = [[None] * LEVELS for _ in range(2)]
    moved = []

    def spread_steps():
        def mm(a, b):
            return jnp.dot(a, b, precision=HIGHEST, preferred_element_type=jnp.float32)

        def centre(l):
            for p in range(2):
                block = x_ref[pl.ds(8 * p + l, members, stride=16), :]
                mean = jnp.sum(block, axis=0, keepdims=True) * (1.0 / members)
                means[p][l] = mean
                pert_ref[p * members : (p + 1) * members, l * PATCH : (l + 1) * PATCH] = block - mean

        squares = jnp.sum(system * system, axis=1, keepdims=True)
        norms = [
            jnp.sqrt(jnp.sum(squares[p * members : (p + 1) * members], axis=0, keepdims=True))
            for p in range(2)
        ]
        first_half = lax.broadcasted_iota(jnp.int32, (both, 1), 0) < members
        norm = jnp.where(first_half, norms[0], norms[1])
        eye = (
            lax.broadcasted_iota(jnp.int32, (both, both), 0)
            == lax.broadcasted_iota(jnp.int32, (both, both), 1)
        ).astype(jnp.float32)
        iterate = system / norm
        root = update = 1.5 * eye - 0.5 * iterate
        for sweep in range(1, NS_ITERS):
            iterate = mm(iterate, update)
            centre(3 * sweep - 3)
            yield
            update = 1.5 * eye - 0.5 * mm(root, iterate)
            centre(3 * sweep - 2)
            yield
            root = mm(update, root)
            if 3 * sweep - 1 < LEVELS:
                centre(3 * sweep - 1)
            yield
        spread = root * jnp.sqrt((members - 1.0) / norm)
        tn = (((0,), (0,)), ((), ()))
        for l in range(LEVELS):
            moved.append(
                lax.dot_general(
                    spread, pert_ref[:, l * PATCH : (l + 1) * PATCH], tn,
                    precision=HIGHEST, preferred_element_type=jnp.float32,
                )
            )
            yield

    m = [m[8 * q : 8 * q + 8, :] for q in range(8)]
    f = [
        jnp.where(left, forcings[0][8 * q : 8 * q + 8, :], forcings[1][8 * q : 8 * q + 8, :])
        for q in range(8)
    ]
    inverse = [[None] * 4 for _ in range(8)]
    steps = spread_steps()

    def spread_row(v, row):
        return jnp.broadcast_to(v[row : row + 1, :], tile)

    for k in range(0, members, 4):
        next(steps, None)
        q, r = divmod(k, 8)
        c = [
            [jnp.take_along_axis(v, jnp.where(left, j, members + j), axis=1, mode="promise_in_bounds") for v in m]
            for j in range(k, k + 4)
        ]
        b = [[spread_row(c[j][q], r + i) for j in range(4)] for i in range(4)]
        det = 1.0 / (b[0][0] * b[1][1] - b[0][1] * b[0][1])
        a00, a01, a11 = b[1][1] * det, -b[0][1] * det, b[0][0] * det
        e00, e01 = a00 * b[0][2] + a01 * b[1][2], a00 * b[0][3] + a01 * b[1][3]
        e10, e11 = a01 * b[0][2] + a11 * b[1][2], a01 * b[0][3] + a11 * b[1][3]
        s00 = b[2][2] - (b[0][2] * e00 + b[1][2] * e10)
        s01 = b[2][3] - (b[0][2] * e01 + b[1][2] * e11)
        s11 = b[3][3] - (b[0][3] * e01 + b[1][3] * e11)
        det = 1.0 / (s00 * s11 - s01 * s01)
        t00, t01, t11 = s11 * det, -s01 * det, s00 * det
        g00, g01 = e00 * t00 + e01 * t01, e00 * t01 + e01 * t11
        g10, g11 = e10 * t00 + e11 * t01, e10 * t01 + e11 * t11
        x01 = a01 + (g00 * e10 + g01 * e11)
        x = [
            [a00 + (g00 * e00 + g01 * e01), x01, -g00, -g01],
            [x01, a11 + (g10 * e10 + g11 * e11), -g10, -g11],
            [-g00, -g10, t00, t01],
            [-g01, -g11, t01, t11],
        ]
        rows = [spread_row(m[q], r + i) for i in range(4)]
        loads = [spread_row(f[q], r + i) for i in range(4)]
        for j in range(4):
            for i in range(4):
                old = inverse[q][j]
                inverse[q][j] = x[i][j] if old is None else jnp.where(sub_id == r + i, x[i][j], old)
        rows = [(x[i][0] * rows[0] + x[i][1] * rows[1]) + (x[i][2] * rows[2] + x[i][3] * rows[3]) for i in range(4)]
        loads = [(x[i][0] * loads[0] + x[i][1] * loads[1]) + (x[i][2] * loads[2] + x[i][3] * loads[3]) for i in range(4)]
        pivot = (sub_id >= r) & (sub_id < r + 4)
        for i in range(4):
            c[i][q] = jnp.where(pivot, 0.0, c[i][q])
        if k < members - 4:
            m = [
                m[n] - ((c[0][n] * rows[0] + c[1][n] * rows[1]) + (c[2][n] * rows[2] + c[3][n] * rows[3]))
                for n in range(8)
            ]
        f = [
            f[n] - ((c[0][n] * loads[0] + c[1][n] * loads[1]) + (c[2][n] * loads[2] + c[3][n] * loads[3]))
            for n in range(8)
        ]
    for _ in steps:
        pass
    weight = []
    for q in range(8):
        terms = [
            inverse[q][j] * jnp.where(sub_id < 4, f[q][j : j + 1, :], f[q][4 + j : 5 + j, :])
            for j in range(4)
        ]
        weight.append((terms[0] + terms[1]) + (terms[2] + terms[3]))
    weight = jnp.concatenate(weight, 0)
    turned = pltpu.roll(weight, members, 1)
    for p in range(2):
        wide = jnp.where(left_all, weight, turned) if p == 0 else jnp.where(left_all, turned, weight)
        for l in range(LEVELS):
            rows = slice(p * members, (p + 1) * members)
            shift = jnp.sum(wide * pert_ref[rows, l * PATCH : (l + 1) * PATCH], axis=0, keepdims=True)
            out_ref[pl.ds(8 * p + l, members, stride=16), :] = moved[l][rows] + (means[p][l] + shift)


def unpack_kernel(x_ref, out_hbm, out_ref, sems):
    copies = []
    for l in range(LEVELS):
        rows = slice(ROWS * l, ROWS * (l + 1))
        for h in range(2):
            cols = slice(h * PATCH, (h + 1) * PATCH)
            base = 8 * h + l
            if TURN:
                out_ref[rows.start : rows.start + TURN, cols] = x_ref[
                    pl.ds(16 * (ROWS - TURN) + base, TURN, stride=16), :
                ]
            out_ref[rows.start + TURN : rows.stop, cols] = x_ref[pl.ds(base, ROWS - TURN, stride=16), :]
        if l % 2:
            some = pl.ds(ROWS * (l - 1), 2 * ROWS)
            copies.append(pltpu.make_async_copy(out_ref.at[some], out_hbm.at[some], sems.at[l // 2]))
            copies[-1].start()
    for copy in copies:
        copy.wait()


VMEM = pl.BlockSpec(memory_space=pltpu.VMEM)
SMEM = pl.BlockSpec(memory_space=pltpu.SMEM)
HBM = pl.BlockSpec(memory_space=pltpu.HBM)


def f32(*dims):
    return jax.ShapeDtypeStruct(dims, jnp.float32)


def call(kernel, outs, specs, scratch=(), flops=1_000_000, name=None, to=VMEM):
    return pl.pallas_call(
        kernel,
        out_shape=outs if len(outs) > 1 else outs[0],
        in_specs=specs,
        out_specs=[to] * len(outs) if len(outs) > 1 else to,
        scratch_shapes=scratch,
        compiler_params=pltpu.CompilerParams(vmem_limit_bytes=VMEM_LIMIT),
        cost_estimate=pl.CostEstimate(flops=flops, bytes_accessed=1_000_000, transcendentals=0),
        name=name,
    )


def exchange(x):
    z, inner = lax.axis_size("grp_0") * lax.axis_size("grp_1"), lax.axis_size("sub") * lax.axis_size("rep")
    groups = [[(g + TURN) % z * inner + i for g in range(z)] for i in range(inner)]
    return lax.all_to_all(x, ("grp_0", "grp_1", "sub", "rep"), 0, 0, axis_index_groups=groups, tiled=True)


def swap_ends(x):
    grp = lax.axis_size("grp_0") * lax.axis_size("grp_1")
    groups = [[2 * (SUBS * g + y) + rep for y in range(SUBS) for rep in (1, 0)] for g in range(grp)]
    return lax.all_to_all(x, ("grp_0", "grp_1", "sub", "rep"), 0, 0, axis_index_groups=groups, tiled=True)


def on_device(start, diffusivity, stability, observed, variance, site, live):
    def vmem(*dims, dtype=jnp.float32):
        return pltpu.VMEM(dims, dtype)

    send = call(
        pack_kernel,
        [f32(2 * SUBS * BLOCK, PATCH)],
        [HBM] * 7,
        scratch=[
            vmem(LEVELS, 8, COLS),
            vmem(LEVELS, 8, COLS),
            vmem(8, COLS),
            vmem(8, COLS),
            vmem(LEVELS, ROWS, PATCH),
            vmem(ROWS, PATCH),
            vmem(1, LEVELS),
            vmem(2, PATCH),
            vmem(2, PATCH),
            vmem(2, PATCH, dtype=jnp.int32),
            vmem(1, 2, dtype=jnp.int32),
            pltpu.SemaphoreType.DMA((11,)),
        ],
        name="pack",
    )(
        *(
            pltpu.with_memory_space_constraint(v, pltpu.HBM)
            for v in (
                start.reshape(LEVELS, ROWS, COLS),
                diffusivity,
                stability,
                observed.reshape(2, PATCH),
                variance.reshape(2, PATCH),
                site.reshape(2, PATCH),
                live,
            )
        )
    )
    got = swap_ends(send.reshape(2 * SUBS, BLOCK, PATCH))
    forecast, slots = call(
        forecast_kernel,
        [f32(ROWS * 16, PATCH), f32(8, PATCH)],
        [VMEM] * 3,
        scratch=[vmem(24 * TALL, PATCH), vmem(24 * TALL, PATCH), vmem(3 * (ROWS + 16), PATCH)],
        name="forecast",
    )(start.reshape(LEVELS * ROWS, COLS), diffusivity, got.reshape(2 * SUBS * BLOCK, PATCH))
    gathered = exchange(forecast.reshape(ROWS, 16, PATCH))
    analysed = call(
        analysis_kernel,
        [f32(MEMBERS * 16, PATCH)],
        [VMEM] * 2,
        scratch=[pltpu.VMEM((2 * MEMBERS, LEVELS * PATCH), jnp.float32)],
        name="analysis",
    )(gathered.reshape(MEMBERS * 16, PATCH), slots)
    returned = exchange(analysed.reshape(MEMBERS, 16, PATCH))
    out = call(
        unpack_kernel,
        [f32(LEVELS * ROWS, COLS)],
        [VMEM],
        scratch=[vmem(LEVELS * ROWS, COLS), pltpu.SemaphoreType.DMA((LEVELS // 2,))],
        name="unpack",
        to=HBM,
    )(
        returned.reshape(ROWS * 16, PATCH)
    )
    return out.reshape(1, LEVELS, ROWS, COLS)


def solution(mesh):
    split = Mesh(
        mesh.devices.reshape(16, 4, mesh.shape["sub"], mesh.shape["rep"]),
        ("grp_0", "grp_1", "sub", "rep"),
    )
    return jax.shard_map(
        on_device,
        mesh=split,
        in_specs=(
            P(GRP, None, "sub", "rep"),
            P("sub", "rep"),
            P(GRP, None),
            P(SUB_GRP, "rep", None),
            P(SUB_GRP, "rep", None),
            P(SUB_GRP, "rep", None),
            P(SUB_GRP, "rep"),
        ),
        out_specs=P(GRP, None, "sub", "rep"),
        check_vma=False,
    )
```
